32 devices in a mesh: groups: 2 (over y), wide: 16 (over z, x, core).
Axes of the slice: x: 2, y: 2, z: 4, core: 2. Of those that a mesh axis runs over, the one named last changes fastest.
Arguments:
- tensor: bfloat16 [1024, 256, 256], P(None, 'wide'), may hold values from -1 to 1
- occupied: bfloat16 [512, 256], P(('groups', 'wide')), parts along dimension 0, may hold values from -0.375 to 0.375
- virtual: bfloat16 [512, 256], P(('groups', 'wide')), parts along dimension 0, may hold values from -0.375 to 0.375
- block_mask: int32 [16, 4, 4], replicated, may hold values 0 or 1
- ri_order: int32 [16], replicated, may hold values from 0 to 15, each once
Outputs:
- polar_blocks: float32 [2048, 64], P(('groups', 'wide')), parts along dimension 0
The draws below stay inside these ranges and needn't reach their ends.
There are 2 independent parts, one for each index of `groups`. The reference program is written for one: setup_inputs(seed, part) draws one part's arguments, and reference() takes and returns one part's arrays. A program takes and returns all parts, laid end to end along the dimension named above; an argument that names none is the same for every part. Nothing has to cross between parts.
All inputs are finite; a program needn't handle non-finite values.
Results may differ from the reference program's by a relative error of at most 0.0041.
Values may be sent and summed in bfloat16 or wider, within the bound.
No kernel may reach another device: no remote copies, remote signals or barrier semaphores. Data moves between devices by JAX's collectives and lax.ppermute only.
A program may use at most 128 MiB of HBM per device.

```python
import jax
import jax.numpy as jnp
from jax import lax

BLK = 64
WIN = 256
NOB = 4
RB = 16
NRI = 1024


def set_ends(entries, rng, smallest, high):
    longest = entries.shape.index(max(entries.shape))
    spots = []
    for shift in (0, 1):
        where = [jax.random.randint(jax.random.fold_in(rng, axis), (), 0, length) for axis, length in enumerate(entries.shape)]
        where[longest] = (where[longest] + shift) % entries.shape[longest]
        spots.append(tuple(where))
    return entries.at[spots[0]].set(smallest).at[spots[1]].set(high)


def block_scale(rng, shape, shards, low, top_value):
    factor_of = 1.0
    for axis_at, shards_of in shards:
        heights = jax.random.uniform(jax.random.fold_in(jax.random.fold_in(rng, 6), axis_at), (shards_of,), jnp.float32, low / len(shards), top_value / len(shards))
        factor_of = factor_of * jnp.repeat(jnp.exp(heights), shape[axis_at] // shards_of).reshape((-1,) + (1,) * (len(shape) - 1 - axis_at))
    return factor_of


def noise(key, extent, deviation, most, cuts=(), kind=jnp.bfloat16):
    drawn = deviation * jax.random.normal(key, extent, jnp.float32)
    if cuts:
        drawn = drawn * block_scale(key, extent, cuts, -0.22, 0.18)
    return jnp.clip(drawn, -most, most).astype(kind)


def setup_inputs(seed: int = 0, part: int = 0) -> dict:
    splits = jax.random.split(jax.random.key(seed), 6)
    own_keys = jax.random.split(jax.random.fold_in(splits[5], part), 6)
    tensor = noise(splits[0], (NRI, WIN, WIN), 0.0625, 1.0, ((1, 16),))
    occupied = noise(own_keys[1], (WIN, WIN), WIN ** -0.5, 0.375, ((0, 16),))
    virtual = noise(own_keys[2], (WIN, WIN), WIN ** -0.5, 0.375, ((0, 16),))
    block_mask = set_ends((jax.random.randint(splits[3], (RB, NOB, NOB), 0, 4) < 3).astype(jnp.int32), jax.random.fold_in(splits[3], 1), 0, 1)
    ri_order = jax.random.permutation(splits[4], RB).astype(jnp.int32)
    return {"tensor": tensor, "occupied": occupied, "virtual": virtual, "block_mask": block_mask, "ri_order": ri_order}


def reference(tensor, occupied, virtual, block_mask, ri_order):
    occ_full = occupied.astype(jnp.float32)
    virt_full = virtual.astype(jnp.float32)

    def one_block(block):
        start = (block * BLK).astype(jnp.int32)
        rows = lax.dynamic_slice_in_dim(tensor, start, BLK, 0)
        kept = lax.dynamic_index_in_dim(block_mask, block, 0, keepdims=False)
        kept_full = jnp.broadcast_to(kept[:, None, :, None] > 0, (NOB, BLK, NOB, BLK)).reshape(WIN, WIN)
        masked = jnp.where(kept_full[None], rows, jnp.zeros((), rows.dtype)).astype(jnp.float32)
        occ_half = jnp.einsum("qln,ns->qls", masked, occ_full).astype(jnp.bfloat16)
        occ_half = lax.optimization_barrier(occ_half).astype(jnp.float32)
        mixed = jnp.einsum("ml,qls->qms", virt_full, occ_half).astype(jnp.bfloat16)
        mixed = lax.optimization_barrier(mixed).astype(jnp.float32)
        return jnp.einsum("pms,qms->pq", masked, mixed)

    blocks = lax.map(one_block, ri_order.astype(jnp.int32))
    return blocks.reshape(NRI, BLK)
```

```python
import jax
import jax.numpy as jnp
from jax import lax
from jax.sharding import PartitionSpec as P

PLANE = 4


def shards(tensor, occupied, virtual, block_mask, ri_order):
    wide_count = lax.axis_size("wide")
    outer = wide_count // PLANE
    me = lax.axis_index("wide")
    group = lax.axis_index("groups")
    plane, lane = me // PLANE, me % PLANE
    ri_total, orb, window = tensor.shape
    rows = ri_total // wide_count
    half = rows // 2
    barrier = lax.optimization_barrier

    planes = [[PLANE * z + i for i in range(PLANE)] for z in range(outer)]

    def inplane(x):
        return lax.all_to_all(
            x, "wide", split_axis=0, concat_axis=0, tiled=True, axis_index_groups=planes
        )

    def shift(x, dz, flip=0):
        pairs = [
            (w, ((w // PLANE + dz) % outer) * PLANE + ((w % PLANE) ^ flip))
            for w in range(wide_count)
        ]
        return lax.ppermute(x, "wide", pairs)

    def swap(x):
        return lax.ppermute(x, "groups", [(0, 1), (1, 0)])

    blocks = tensor.reshape(wide_count, rows, orb, window)

    def part(dz, target, low, count):
        at = ri_order[((plane + dz) % outer) * PLANE + target]
        return lax.dynamic_slice(blocks, (at, low, 0, 0), (1, count, orb, window))[0]

    def parts(dz, low, count):
        return jnp.stack([part(dz, i, low, count) for i in range(PLANE)])

    own_low, other_low = group * half, (1 - group) * half
    order = [d for d in range(1, outer) if d != outer // 2] + [outer // 2]
    first, last = order[0], order[-1]
    steps = [(d, 0, half) for d in order[:-1]]
    steps += [(last, 0, half // 2), (last, half // 2, half // 2)]

    dens = jnp.stack([occupied, virtual])
    own, other = {}, {}
    dens_from = [dens]
    state = {}

    pieces = [part(first, lane ^ q, own_low, half) for q in range(PLANE)]
    sent = [shift(p, first, q) for q, p in enumerate(pieces)]
    small = [shift(dens, d) for d in range(1, outer)]
    ready = inplane(parts(steps[1][0], own_low + steps[1][1], steps[1][2]))
    out = barrier((tensor, ready, *sent, *small))
    tensor, ready = out[0], out[1]
    arrived = jnp.stack(out[2 : 2 + PLANE])
    dens_from += list(out[2 + PLANE :])
    blocks = tensor.reshape(wide_count, rows, orb, window)
    own[steps[0]] = arrived

    for k in range(1, len(steps)):
        z_out = shift(ready, steps[k][0])
        y_out = swap(arrived)
        extra = []
        if k + 1 < len(steps):
            nxt = steps[k + 1]
            extra.append(inplane(parts(nxt[0], own_low + nxt[1], nxt[2])))
        if k == 1:
            extra.append(inplane(jnp.broadcast_to(jnp.stack(dens_from)[None], (PLANE, outer, 2, orb, window))))
        if k == len(steps) - 2:
            extra.append(inplane(parts(0, own_low, half)))
        if k == len(steps) - 1:
            extra.append(inplane(parts(0, other_low, half)))
        out = list(barrier((tensor, z_out, y_out, *extra)))
        tensor, arrived_z, y_res = out[0], out[1], out[2]
        extra = out[3:]
        blocks = tensor.reshape(wide_count, rows, orb, window)
        if k + 1 < len(steps):
            ready = extra.pop(0)
        if k == 1:
            dens_all = extra.pop(0)
        if k == len(steps) - 2:
            own[(0, 0, half)] = extra.pop(0)
        if k == len(steps) - 1:
            other[(0, 0, half)] = extra.pop(0)
        other[steps[k - 1]] = y_res
        arrived = arrived_z
        own[steps[k]] = arrived
    final_y = swap(arrived)

    def lay(x):
        return jnp.swapaxes(x, 0, 1).reshape(x.shape[1], PLANE * orb, window)

    quarter = half // 2
    shifts = [0] + order
    own_rows = [own[(d, 0, half)] for d in shifts[:-1]]
    own_rows.append(jnp.concatenate([own[steps[-2]], own[steps[-1]]], axis=1))
    other_rows = [other[(d, 0, half)] for d in shifts[:-1]]
    m_own = jnp.concatenate([lay(x) for x in own_rows], axis=1)
    m_oth = jnp.concatenate(
        [lay(x[:, :quarter]) for x in other_rows] + [lay(other[steps[-2]])], axis=1
    )
    m_last = jnp.concatenate([lay(x[:, quarter:]) for x in other_rows] + [lay(final_y)], axis=1)

    source = []
    for d in shifts:
        for i in range(PLANE):
            who = (lane ^ i) if d == first else i
            source.append(((plane - d) % outer) * PLANE + who)
    source = jnp.stack(source)
    orbital = (source[:, None] * orb + jnp.arange(orb)[None, :]).reshape(window)

    by_source = dens_all.transpose(2, 1, 0, 3, 4)
    back = (plane - jnp.arange(outer)) % outer
    occ = jnp.take(by_source[0], back, axis=0).reshape(window, window)
    vir = jnp.take(by_source[1], back, axis=0).reshape(window, window)
    vir = jnp.take(jnp.take(vir, orbital, axis=0), orbital, axis=1)

    block = ri_order[me]
    keep = jnp.take(block_mask[block], orbital // rows, axis=0)
    keep = jnp.repeat(keep, rows, axis=1) > 0

    def mix(m):
        m = jnp.where(keep[None], m, jnp.zeros((), m.dtype))
        h = jnp.einsum("qln,ns->qls", m, occ, preferred_element_type=jnp.float32).astype(m.dtype)
        x = jnp.einsum("ml,qls->qms", vir, h, preferred_element_type=jnp.float32).astype(m.dtype)
        return m, x

    masked, mixed = zip(mix(m_own), mix(m_oth), mix(m_last))
    masked, mixed = jnp.concatenate(masked), jnp.concatenate(mixed)
    polar = jnp.einsum("pms,qms->pq", masked, mixed, preferred_element_type=jnp.float32)
    turned = jnp.roll(polar, (half, half), (0, 1))
    return jnp.where(group == 0, polar, turned)


def solution(mesh):
    in_specs = (
        P(None, "wide", None),
        P(("groups", "wide"), None),
        P(("groups", "wide"), None),
        P(),
        P(),
    )
    out_specs = P(("groups", "wide"), None)
    return jax.shard_map(shards, mesh=mesh, in_specs=in_specs, out_specs=out_specs, check_vma=False)
```

```python
import functools

import jax
import jax.numpy as jnp
from jax import lax
from jax.experimental import pallas as pl
from jax.experimental.pallas import tpu as pltpu
from jax.sharding import PartitionSpec as P

PLANE = 4
ROWS = 16
VMEM = pl.BlockSpec(memory_space=pltpu.VMEM)
SMEM = pl.BlockSpec(memory_space=pltpu.SMEM)
HBM = pl.BlockSpec(memory_space=pl.ANY)
DOT = functools.partial(jnp.dot, preferred_element_type=jnp.float32)


def gather_kernel(plan, outer, half, count, order_ref, blocks_ref, *rest):
    outs, sems = rest[:count], rest[count]
    me = lax.axis_index("wide")
    group = lax.axis_index("groups")
    plane, lane = me // PLANE, me % PLANE
    copies = []
    for n, (out, place, dz, target, flip, start, rows, own) in enumerate(plan):
        who = (lane ^ target) if flip else target
        block = order_ref[lax.rem(plane + dz, outer) * PLANE + who]
        low = (group if own else 1 - group) * half + start
        to = outs[out] if place is None else outs[out].at[place[0], pl.ds(place[1], rows)]
        copies.append(
            pltpu.make_async_copy(blocks_ref.at[block, pl.ds(low, rows)], to, sems.at[n])
        )
    for copy in copies:
        copy.start()
    for copy in copies:
        copy.wait()


def gather(plan, shapes, outer, half, ri_order, blocks):
    size = sum(s.size for s in shapes) * 4
    return pl.pallas_call(
        functools.partial(gather_kernel, plan, outer, half, len(shapes)),
        out_shape=shapes,
        in_specs=[SMEM, HBM],
        out_specs=[HBM] * len(shapes),
        scratch_shapes=[pltpu.SemaphoreType.DMA((len(plan),))],
        cost_estimate=pl.CostEstimate(flops=0, bytes_accessed=size, transcendentals=0),
    )(ri_order, blocks)


def load(pieces, held, sems, base=0):
    groups = {}
    n = base
    for ref, lead, low, rows, to, at in pieces:
        src = ref if lead is None else ref.at[lead]
        height = src.shape[1]
        for r in range(0, rows, ROWS):
            copy = pltpu.make_async_copy(
                src.at[pl.ds(low + r, ROWS)],
                held.at[pl.ds(to + r, ROWS), pl.ds(at, height)],
                sems.at[n],
            )
            groups.setdefault((to + r) // ROWS, []).append(copy)
            n += 1
    for g in sorted(groups):
        for copy in groups[g]:
            copy.start()
    return groups


def half_step(held, first, occ, vir, keep, mask_t, mix_t, to):
    window = occ.shape[0]
    m = held[first : first + ROWS] * keep[None]
    mask_t[:, to : to + ROWS, :] = jnp.swapaxes(m, 0, 1)
    h = DOT(m.reshape(ROWS * window, window), occ).astype(jnp.bfloat16)
    mixed = [
        DOT(vir, h[p * window : (p + 1) * window]).astype(jnp.bfloat16)[None] for p in range(ROWS)
    ]
    mix_t[:, to : to + ROWS, :] = jnp.swapaxes(jnp.concatenate(mixed), 0, 1)


def front_kernel(places, shifts, outer, orb, count, order_ref, mask_ref, dens_ref, *rest):
    refs = rest[:count]
    mask_t, mix_t, occ_ref, vir_ref, keep_ref, held, sems = rest[count:]
    pieces = [(refs[p[0]],) + p[1:] for p in places]
    groups = load(pieces, held, sems)
    me = lax.axis_index("wide")
    plane, lane = me // PLANE, me % PLANE
    window = occ_ref.shape[0]
    nblk = mask_ref.shape[2]
    block_rows = window // nblk

    def assembled(shape, dim):
        at = lax.broadcasted_iota(jnp.int32, shape, dim)
        place = at // (PLANE * orb)
        device = (at // orb) % PLANE
        source = jnp.zeros(shape, jnp.int32)
        for n, dz in enumerate(shifts):
            who = (device ^ lane) if n == 1 else device
            from_plane = lax.rem(plane + (outer - dz), outer)
            source = jnp.where(place == n, from_plane * PLANE + who, source)
        return source * orb + at % orb

    arrived = lax.broadcasted_iota(jnp.int32, (window, 2 * window), 1)
    kind = (arrived // orb) % 2
    dz = (arrived // (2 * orb)) % outer
    device = arrived // (2 * orb * outer)
    source = lax.rem(plane - dz + outer, outer) * PLANE + device
    orbital = source * orb + arrived % orb
    rows = lax.broadcasted_iota(jnp.int32, (window, 2 * window), 0)
    pick = jnp.where((rows == orbital) & (kind == 0), 1.0, 0.0).astype(jnp.bfloat16)
    dens = dens_ref[...]
    occ = DOT(pick, dens).astype(jnp.bfloat16)
    pick = (assembled((window, 2 * window), 0) == orbital) & (kind == 1)
    pick = jnp.where(pick, 1.0, 0.0).astype(jnp.bfloat16)
    vir = DOT(pick, dens).astype(jnp.bfloat16)
    rows = lax.broadcasted_iota(jnp.int32, (window, window), 0)
    pick = jnp.where(rows == assembled((window, window), 1), 1.0, 0.0).astype(jnp.bfloat16)
    vir = DOT(vir, pick).astype(jnp.bfloat16)
    block = order_ref[me]
    lam = assembled((window, window), 0) // block_rows
    sig = lax.broadcasted_iota(jnp.int32, (window, window), 1) // block_rows
    keep = jnp.zeros((window, window), jnp.int32)
    for a in range(nblk):
        for b in range(nblk):
            keep = jnp.where((lam == a) & (sig == b), mask_ref[block, a, b], keep)
    keep = jnp.where(keep > 0, 1.0, 0.0).astype(jnp.bfloat16)
    occ_ref[...] = occ
    vir_ref[...] = vir
    keep_ref[...] = keep
    for g in sorted(groups):
        for copy in groups[g]:
            copy.wait()
        half_step(held, g * ROWS, occ, vir, keep, mask_t, mix_t, g * ROWS)


def back_kernel(places, count, occ_ref, vir_ref, keep_ref, front_mask, front_mix, *rest):
    refs = rest[:count]
    out_ref, mask_t, mix_t, held, sems = rest[count:]
    done = front_mask.shape[1]
    pieces = [(refs[p[0]],) + p[1:] for p in places]
    groups = load(pieces, held, sems, 2)
    first = pltpu.make_async_copy(front_mask, mask_t.at[:, pl.ds(0, done)], sems.at[0])
    second = pltpu.make_async_copy(front_mix, mix_t.at[:, pl.ds(0, done)], sems.at[1])
    first.start()
    second.start()
    occ, vir, keep = occ_ref[...], vir_ref[...], keep_ref[...]
    for g in sorted(groups):
        for copy in groups[g]:
            copy.wait()
        half_step(held, g * ROWS, occ, vir, keep, mask_t, mix_t, done + g * ROWS)
    first.wait()
    second.wait()
    window, rows = mask_t.shape[0], mask_t.shape[1]
    deep = 16

    def body(step, total):
        for k in range(deep):
            m = step * deep + k
            total += lax.dot_general(
                mask_t[m], mix_t[m], (((1,), (1,)), ((), ())), preferred_element_type=jnp.float32
            )
        return total

    total = lax.fori_loop(0, window // deep, body, jnp.zeros((rows, rows), jnp.float32))
    half = rows // 2
    turned = jnp.concatenate([total[half:], total[:half]], axis=0)
    turned = jnp.concatenate([turned[:, half:], turned[:, :half]], axis=1)
    out_ref[...] = jnp.where(lax.axis_index("groups") == 0, total, turned)


def shards(tensor, occupied, virtual, block_mask, ri_order):
    wide_count = lax.axis_size("wide")
    outer = wide_count // PLANE
    ri_total, orb, window = tensor.shape
    rows = ri_total // wide_count
    half = rows // 2
    quarter = half // 2
    kind = tensor.dtype
    barrier = lax.optimization_barrier
    planes = [[PLANE * z + i for i in range(PLANE)] for z in range(outer)]

    def inplane(x):
        return lax.all_to_all(
            x, "wide", split_axis=0, concat_axis=0, tiled=True, axis_index_groups=planes
        )

    def shift(x, dz, flip=0):
        pairs = [
            (w, ((w // PLANE + dz) % outer) * PLANE + ((w % PLANE) ^ flip))
            for w in range(wide_count)
        ]
        return lax.ppermute(x, "wide", pairs)

    def swap(x):
        return lax.ppermute(x, "groups", [(0, 1), (1, 0)])

    order = [d for d in range(1, outer) if d != outer // 2] + [outer // 2]
    first, last = order[0], order[-1]
    shape = lambda *s: jax.ShapeDtypeStruct(s + (orb, window), kind)
    blocks = tensor.reshape(wide_count, rows, orb, window)

    plan = [(q, None, first, q, True, 0, half, True) for q in range(PLANE)]
    pieces = gather(plan, [shape(half)] * PLANE, outer, half, ri_order, blocks)
    held_back, *pieces = barrier((blocks, *pieces))
    plan, shapes = [], []
    for d in order[1:]:
        plan += [(len(shapes), (i, 0), d, i, False, 0, half, True) for i in range(PLANE)]
        shapes.append(shape(PLANE, half))
    for own in (True, False):
        low = 0 if own else half
        plan += [(len(shapes), (i, low), 0, i, False, 0, half, own) for i in range(PLANE)]
    shapes.append(shape(PLANE, rows))
    *to_send, to_near = gather(plan, shapes, outer, half, ri_order, held_back)

    base = jnp.stack([occupied, virtual])
    dens, small = [base], list(range(1, outer))
    per_phase = -(-len(small) // (outer - 2))
    own_in, swapped = [], []
    for k in range(outer):
        if k == 0:
            moved = [shift(p, first, q) for q, p in enumerate(pieces)]
        elif k <= outer - 3:
            moved = [shift(ready, order[k])]
        else:
            moved = [shift(ready[k - outer + 2], last)]
        turn = [swap(own_in[-1])] if k else []
        tiny, near_by = [], []
        if 1 <= k <= outer - 2:
            tiny = [shift(base, d) for d in small[:per_phase]]
            small = small[per_phase:]
        if k <= outer - 3:
            near_by = [inplane(to_send[k])]
        elif k == outer - 2:
            near = inplane(to_near)
        else:
            spread = jnp.broadcast_to(jnp.stack(dens)[None], (PLANE, outer, 2, orb, window))
            near_by = [inplane(spread), near]
        moved, turn, tiny, near_by, to_send, to_near, base = barrier(
            (moved, turn, tiny, near_by, to_send, to_near, base)
        )
        own_in.append(moved[0] if k else jnp.stack(moved))
        swapped += turn
        dens += tiny
        if k <= outer - 3:
            ready = near_by[0]
            if k == outer - 3:
                ready = [ready[:, :quarter], ready[:, quarter:]]
    dens_all, near = near_by
    swapped.append(swap(own_in[-1]))

    front, back = [], []
    for i in range(PLANE):
        for n in range(outer):
            at = (n * PLANE + i) * orb
            if n == 0:
                front += [(near, i, 0, half + quarter, 0, at)]
                back += [(near, i, half + quarter, quarter, 0, at)]
            elif n < outer - 1:
                front += [(own_in[n - 1], i, 0, half, 0, at)]
                front += [(swapped[n - 1], i, 0, quarter, half, at)]
                back += [(swapped[n - 1], i, quarter, quarter, 0, at)]
            else:
                front += [(own_in[-2], i, 0, quarter, 0, at)]
                front += [(own_in[-1], i, 0, quarter, quarter, at)]
                front += [(swapped[-2], i, 0, quarter, half, at)]
                back += [(swapped[-1], i, 0, quarter, 0, at)]

    def places(listed):
        if orb % ROWS == 0:
            arrays = []
            for p in listed:
                if not any(p[0] is a for a in arrays):
                    arrays.append(p[0])
            number = lambda x: [x is a for a in arrays].index(True)
            return [(number(p[0]),) + p[1:] for p in listed], arrays
        size = max(p[4] + p[3] for p in listed)
        whole = []
        for r in range(0, size, ROWS):
            row = sorted((p for p in listed if p[4] <= r < p[4] + p[3]), key=lambda p: p[5])
            cut = [lax.slice_in_dim(p[0][p[1]], p[2] + r - p[4], p[2] + r - p[4] + ROWS) for p in row]
            whole.append(jnp.concatenate(cut, axis=1))
        return [(0, None, 0, size, 0, 0)], [jnp.concatenate(whole)]

    def copies(table):
        return sum(p[3] // ROWS for p in table)

    params = pltpu.CompilerParams(vmem_limit_bytes=48 * 2**20)
    table, arrays = places(front)
    done = half + quarter
    mat = jax.ShapeDtypeStruct((window, window), kind)
    tall = jax.ShapeDtypeStruct((window, done, window), kind)
    front_mask, front_mix, occ, vir, keep = pl.pallas_call(
        functools.partial(front_kernel, table, [0] + order, outer, orb, len(arrays)),
        out_shape=[tall, tall, mat, mat, mat],
        in_specs=[SMEM, SMEM, VMEM] + [HBM] * len(arrays),
        out_specs=[VMEM] * 5,
        scratch_shapes=[
            pltpu.VMEM((done, window, window), kind),
            pltpu.SemaphoreType.DMA((copies(table),)),
        ],
        compiler_params=params,
        cost_estimate=pl.CostEstimate(
            flops=4 * done * window**3, bytes_accessed=6 * done * window**2, transcendentals=0
        ),
    )(ri_order, block_mask, dens_all.reshape(2 * window, window), *arrays)
    table, arrays = places(back)
    return pl.pallas_call(
        functools.partial(back_kernel, table, len(arrays)),
        out_shape=jax.ShapeDtypeStruct((rows, rows), jnp.float32),
        in_specs=[VMEM] * 3 + [HBM] * (2 + len(arrays)),
        out_specs=VMEM,
        scratch_shapes=[
            pltpu.VMEM((window, rows, window), kind),
            pltpu.VMEM((window, rows, window), kind),
            pltpu.VMEM((quarter, window, window), kind),
            pltpu.SemaphoreType.DMA((2 + copies(table),)),
        ],
        compiler_params=params,
        cost_estimate=pl.CostEstimate(
            flops=4 * quarter * window**3, bytes_accessed=4 * rows * window**2, transcendentals=0
        ),
    )(occ, vir, keep, front_mask, front_mix, *arrays)


def solution(mesh):
    in_specs = (
        P(None, "wide", None),
        P(("groups", "wide"), None),
        P(("groups", "wide"), None),
        P(),
        P(),
    )
    out_specs = P(("groups", "wide"), None)
    return jax.shard_map(shards, mesh=mesh, in_specs=in_specs, out_specs=out_specs, check_vma=False)
```

```python
import functools

import jax
import jax.numpy as jnp
from jax import lax
from jax.experimental import pallas as pl
from jax.experimental.pallas import tpu as pltpu
from jax.sharding import PartitionSpec as P

PLANE = 4
ROWS = 16
VMEM = pl.BlockSpec(memory_space=pltpu.VMEM)
SMEM = pl.BlockSpec(memory_space=pltpu.SMEM)
HBM = pl.BlockSpec(memory_space=pl.ANY)
DOT = functools.partial(jnp.dot, preferred_element_type=jnp.float32)


def gather_kernel(plan, outer, half, count, order_ref, blocks_ref, *rest):
    outs, sems = rest[:count], rest[count]
    me = lax.axis_index("wide")
    group = lax.axis_index("groups")
    plane, lane = me // PLANE, me % PLANE
    copies = []
    for n, (out, place, dz, target, flip, start, rows, own) in enumerate(plan):
        who = (lane ^ target) if flip else target
        block = order_ref[lax.rem(plane + dz, outer) * PLANE + who]
        low = (group if own else 1 - group) * half + start
        to = outs[out] if place is None else outs[out].at[place[0], pl.ds(place[1], rows)]
        copies.append(
            pltpu.make_async_copy(blocks_ref.at[block, pl.ds(low, rows)], to, sems.at[n])
        )
    for copy in copies:
        copy.start()
    for copy in copies:
        copy.wait()


def gather(plan, shapes, outer, half, ri_order, blocks):
    size = sum(s.size for s in shapes) * 4
    return pl.pallas_call(
        functools.partial(gather_kernel, plan, outer, half, len(shapes)),
        out_shape=shapes,
        in_specs=[SMEM, HBM],
        out_specs=[VMEM] * len(shapes),
        compiler_params=pltpu.CompilerParams(vmem_limit_bytes=24 * 2**20),
        scratch_shapes=[pltpu.SemaphoreType.DMA((len(plan),))],
        cost_estimate=pl.CostEstimate(flops=0, bytes_accessed=size, transcendentals=0),
    )(ri_order, blocks)


def load(pieces, held, sems, base=0):
    groups = {}
    n = base
    for ref, lead, low, rows, to, at in pieces:
        src = ref if lead is None else ref.at[lead]
        height = src.shape[1]
        for r in range(0, rows, ROWS):
            copy = pltpu.make_async_copy(
                src.at[pl.ds(low + r, ROWS)],
                held.at[pl.ds(to + r, ROWS), pl.ds(at, height)],
                sems.at[n],
            )
            groups.setdefault((to + r) // ROWS, []).append(copy)
            n += 1
    for g in sorted(groups):
        for copy in groups[g]:
            copy.start()
    return groups


def half_step(held, first, occ, vir, keep, mask_t, mix_t, to):
    window = occ.shape[0]
    m = held[first : first + ROWS] * keep[None]
    mask_t[:, to : to + ROWS, :] = jnp.swapaxes(m, 0, 1)
    h = DOT(m.reshape(ROWS * window, window), occ).astype(jnp.bfloat16)
    mixed = [
        DOT(vir, h[p * window : (p + 1) * window]).astype(jnp.bfloat16)[None] for p in range(ROWS)
    ]
    mix_t[:, to : to + ROWS, :] = jnp.swapaxes(jnp.concatenate(mixed), 0, 1)


def front_kernel(places, shifts, outer, orb, count, order_ref, mask_ref, dens_ref, *rest):
    refs = rest[:count]
    mask_t, mix_t, occ_ref, vir_ref, keep_ref, held, sems = rest[count:]
    pieces = [(refs[p[0]],) + p[1:] for p in places]
    groups = load(pieces, held, sems)
    me = lax.axis_index("wide")
    plane, lane = me // PLANE, me % PLANE
    window = occ_ref.shape[0]
    nblk = mask_ref.shape[2]
    block_rows = window // nblk

    def assembled(shape, dim):
        at = lax.broadcasted_iota(jnp.int32, shape, dim)
        place = at // (PLANE * orb)
        device = (at // orb) % PLANE
        source = jnp.zeros(shape, jnp.int32)
        for n, dz in enumerate(shifts):
            who = (device ^ lane) if n == 1 else device
            from_plane = lax.rem(plane + (outer - dz), outer)
            source = jnp.where(place == n, from_plane * PLANE + who, source)
        return source * orb + at % orb

    arrived = lax.broadcasted_iota(jnp.int32, (window, 2 * window), 1)
    kind = (arrived // orb) % 2
    dz = (arrived // (2 * orb)) % outer
    device = arrived // (2 * orb * outer)
    source = lax.rem(plane - dz + outer, outer) * PLANE + device
    orbital = source * orb + arrived % orb
    rows = lax.broadcasted_iota(jnp.int32, (window, 2 * window), 0)
    pick = jnp.where((rows == orbital) & (kind == 0), 1.0, 0.0).astype(jnp.bfloat16)
    dens = dens_ref[...]
    occ = DOT(pick, dens).astype(jnp.bfloat16)
    pick = (assembled((window, 2 * window), 0) == orbital) & (kind == 1)
    pick = jnp.where(pick, 1.0, 0.0).astype(jnp.bfloat16)
    vir = DOT(pick, dens).astype(jnp.bfloat16)
    rows = lax.broadcasted_iota(jnp.int32, (window, window), 0)
    pick = jnp.where(rows == assembled((window, window), 1), 1.0, 0.0).astype(jnp.bfloat16)
    vir = DOT(vir, pick).astype(jnp.bfloat16)
    block = order_ref[me]
    lam = assembled((window, window), 0) // block_rows
    sig = lax.broadcasted_iota(jnp.int32, (window, window), 1) // block_rows
    keep = jnp.zeros((window, window), jnp.int32)
    for a in range(nblk):
        for b in range(nblk):
            keep = jnp.where((lam == a) & (sig == b), mask_ref[block, a, b], keep)
    keep = jnp.where(keep > 0, 1.0, 0.0).astype(jnp.bfloat16)
    occ_ref[...] = occ
    vir_ref[...] = vir
    keep_ref[...] = keep
    for g in sorted(groups):
        for copy in groups[g]:
            copy.wait()
        half_step(held, g * ROWS, occ, vir, keep, mask_t, mix_t, g * ROWS)


def back_kernel(places, count, occ_ref, vir_ref, keep_ref, front_mask, front_mix, *rest):
    refs = rest[:count]
    out_ref, mask_t, mix_t, held, sems = rest[count:]
    done = front_mask.shape[1]
    pieces = [(refs[p[0]],) + p[1:] for p in places]
    groups = load(pieces, held, sems, 2)
    first = pltpu.make_async_copy(front_mask, mask_t.at[:, pl.ds(0, done)], sems.at[0])
    second = pltpu.make_async_copy(front_mix, mix_t.at[:, pl.ds(0, done)], sems.at[1])
    first.start()
    second.start()
    occ, vir, keep = occ_ref[...], vir_ref[...], keep_ref[...]
    for g in sorted(groups):
        for copy in groups[g]:
            copy.wait()
        half_step(held, g * ROWS, occ, vir, keep, mask_t, mix_t, done + g * ROWS)
    first.wait()
    second.wait()
    window, rows = mask_t.shape[0], mask_t.shape[1]
    deep = 16

    def body(step, total):
        for k in range(deep):
            m = step * deep + k
            total += lax.dot_general(
                mask_t[m], mix_t[m], (((1,), (1,)), ((), ())), preferred_element_type=jnp.float32
            )
        return total

    total = lax.fori_loop(0, window // deep, body, jnp.zeros((rows, rows), jnp.float32))
    half = rows // 2
    turned = jnp.concatenate([total[half:], total[:half]], axis=0)
    turned = jnp.concatenate([turned[:, half:], turned[:, :half]], axis=1)
    out_ref[...] = jnp.where(lax.axis_index("groups") == 0, total, turned)


def shards(tensor, occupied, virtual, block_mask, ri_order):
    wide_count = lax.axis_size("wide")
    outer = wide_count // PLANE
    ri_total, orb, window = tensor.shape
    rows = ri_total // wide_count
    half = rows // 2
    quarter = half // 2
    kind = tensor.dtype
    barrier = lax.optimization_barrier
    planes = [[PLANE * z + i for i in range(PLANE)] for z in range(outer)]

    def inplane(x):
        return lax.all_to_all(
            x, "wide", split_axis=0, concat_axis=0, tiled=True, axis_index_groups=planes
        )

    def shift(x, dz, flip=0):
        pairs = [
            (w, ((w // PLANE + dz) % outer) * PLANE + ((w % PLANE) ^ flip))
            for w in range(wide_count)
        ]
        return lax.ppermute(x, "wide", pairs)

    def swap(x):
        return lax.ppermute(x, "groups", [(0, 1), (1, 0)])

    order = [d for d in range(1, outer) if d != outer // 2] + [outer // 2]
    first, last = order[0], order[-1]
    shape = lambda *s: jax.ShapeDtypeStruct(s + (orb, window), kind)
    blocks = tensor.reshape(wide_count, rows, orb, window)

    plan = [(q, None, first, q, True, 0, half, True) for q in range(PLANE)]
    pieces = gather(plan, [shape(half)] * PLANE, outer, half, ri_order, blocks)
    held_back, *pieces = barrier((blocks, *pieces))
    plan, shapes = [], []
    for d in order[1:]:
        plan += [(len(shapes), (i, 0), d, i, False, 0, half, True) for i in range(PLANE)]
        shapes.append(shape(PLANE, half))
    for own in (True, False):
        low = 0 if own else half
        plan += [(len(shapes), (i, low), 0, i, False, 0, half, own) for i in range(PLANE)]
    shapes.append(shape(PLANE, rows))
    *to_send, to_near = gather(plan, shapes, outer, half, ri_order, held_back)

    base = jnp.stack([occupied, virtual])
    dens, small = [base], list(range(1, outer))
    per_phase = -(-len(small) // max(1, outer - 3))
    own_in, swapped = [], []
    for k in range(outer):
        if k == 0:
            moved = [shift(p, first, q) for q, p in enumerate(pieces)]
        elif k <= outer - 3:
            moved = [shift(ready, order[k])]
        else:
            moved = [shift(ready[k - outer + 2], last)]
        turn = [swap(own_in[-1])] if k else []
        tiny, near_by = [], []
        if 1 <= k <= outer - 2:
            tiny = [shift(base, d) for d in small[:per_phase]]
            small = small[per_phase:]
        if k <= outer - 3:
            near_by = [inplane(to_send[k])]
        elif k == outer - 2:
            near_by = [inplane(to_near)]
        else:
            spread = jnp.broadcast_to(jnp.stack(dens)[None], (PLANE, outer, 2, orb, window))
            near_by = [inplane(spread)]
        moved, turn, tiny, near_by, to_send, to_near, base = barrier(
            (moved, turn, tiny, near_by, to_send, to_near, base)
        )
        own_in.append(moved[0] if k else jnp.stack(moved))
        swapped += turn
        dens += tiny
        if k <= outer - 3:
            ready = near_by[0]
            if k == outer - 3:
                ready = [ready[:, :quarter], ready[:, quarter:]]
        elif k == outer - 2:
            near = near_by[0]
    dens_all = near_by[0]
    swapped.append(swap(own_in[-1]))

    front, back = [], []
    for i in range(PLANE):
        for n in range(outer):
            at = (n * PLANE + i) * orb
            if n == 0:
                front += [(near, i, 0, half + quarter, 0, at)]
                back += [(near, i, half + quarter, quarter, 0, at)]
            elif n < outer - 1:
                front += [(own_in[n - 1], i, 0, half, 0, at)]
                front += [(swapped[n - 1], i, 0, quarter, half, at)]
                back += [(swapped[n - 1], i, quarter, quarter, 0, at)]
            else:
                front += [(own_in[-2], i, 0, quarter, 0, at)]
                front += [(own_in[-1], i, 0, quarter, quarter, at)]
                front += [(swapped[-2], i, 0, quarter, half, at)]
                back += [(swapped[-1], i, 0, quarter, 0, at)]

    def places(listed):
        if orb % ROWS == 0:
            arrays = []
            for p in listed:
                if not any(p[0] is a for a in arrays):
                    arrays.append(p[0])
            number = lambda x: [x is a for a in arrays].index(True)
            return [(number(p[0]),) + p[1:] for p in listed], arrays
        size = max(p[4] + p[3] for p in listed)
        whole = []
        for r in range(0, size, ROWS):
            row = sorted((p for p in listed if p[4] <= r < p[4] + p[3]), key=lambda p: p[5])
            cut = [lax.slice_in_dim(p[0][p[1]], p[2] + r - p[4], p[2] + r - p[4] + ROWS) for p in row]
            whole.append(jnp.concatenate(cut, axis=1))
        return [(0, None, 0, size, 0, 0)], [jnp.concatenate(whole)]

    def copies(table):
        return sum(p[3] // ROWS for p in table)

    params = pltpu.CompilerParams(vmem_limit_bytes=58 * 2**20)
    table, arrays = places(front)
    done = half + quarter
    mat = jax.ShapeDtypeStruct((window, window), kind)
    tall = jax.ShapeDtypeStruct((window, done, window), kind)
    front_mask, front_mix, occ, vir, keep = pl.pallas_call(
        functools.partial(front_kernel, table, [0] + order, outer, orb, len(arrays)),
        out_shape=[tall, tall, mat, mat, mat],
        in_specs=[SMEM, SMEM, VMEM] + [HBM] * len(arrays),
        out_specs=[VMEM] * 5,
        scratch_shapes=[
            pltpu.VMEM((done, window, window), kind),
            pltpu.SemaphoreType.DMA((copies(table),)),
        ],
        compiler_params=params,
        cost_estimate=pl.CostEstimate(
            flops=4 * done * window**3, bytes_accessed=6 * done * window**2, transcendentals=0
        ),
    )(ri_order, block_mask, dens_all.reshape(2 * window, window), *arrays)
    table, arrays = places(back)
    return pl.pallas_call(
        functools.partial(back_kernel, table, len(arrays)),
        out_shape=jax.ShapeDtypeStruct((rows, rows), jnp.float32),
        in_specs=[VMEM] * 3 + [HBM] * (2 + len(arrays)),
        out_specs=VMEM,
        scratch_shapes=[
            pltpu.VMEM((window, rows, window), kind),
            pltpu.VMEM((window, rows, window), kind),
            pltpu.VMEM((quarter, window, window), kind),
            pltpu.SemaphoreType.DMA((2 + copies(table),)),
        ],
        compiler_params=params,
        cost_estimate=pl.CostEstimate(
            flops=4 * quarter * window**3, bytes_accessed=4 * rows * window**2, transcendentals=0
        ),
    )(occ, vir, keep, front_mask, front_mix, *arrays)


def solution(mesh):
    in_specs = (
        P(None, "wide", None),
        P(("groups", "wide"), None),
        P(("groups", "wide"), None),
        P(),
        P(),
    )
    out_specs = P(("groups", "wide"), None)
    return jax.shard_map(shards, mesh=mesh, in_specs=in_specs, out_specs=out_specs, check_vma=False)
```

```python
import functools

import jax
import jax.numpy as jnp
from jax import lax
from jax.experimental import pallas as pl
from jax.experimental.pallas import tpu as pltpu
from jax.sharding import PartitionSpec as P

PLANE = 4
ROWS = 16
VMEM = pl.BlockSpec(memory_space=pltpu.VMEM)
SMEM = pl.BlockSpec(memory_space=pltpu.SMEM)
HBM = pl.BlockSpec(memory_space=pl.ANY)
DOT = functools.partial(jnp.dot, preferred_element_type=jnp.float32)


def gather_kernel(plan, outer, half, count, order_ref, blocks_ref, *rest):
    outs, sems = rest[:count], rest[count]
    me = lax.axis_index("wide")
    group = lax.axis_index("groups")
    plane, lane = me // PLANE, me % PLANE
    copies = []
    for n, (out, place, dz, target, flip, start, rows, own) in enumerate(plan):
        who = (lane ^ target) if flip else target
        block = order_ref[lax.rem(plane + dz, outer) * PLANE + who]
        low = (group if own else 1 - group) * half + start
        to = outs[out] if place is None else outs[out].at[place[0], pl.ds(place[1], rows)]
        copies.append(
            pltpu.make_async_copy(blocks_ref.at[block, pl.ds(low, rows)], to, sems.at[n])
        )
    for copy in copies:
        copy.start()
    for copy in copies:
        copy.wait()


def gather(plan, shapes, outer, half, ri_order, blocks):
    size = sum(s.size for s in shapes) * 4
    return pl.pallas_call(
        functools.partial(gather_kernel, plan, outer, half, len(shapes)),
        out_shape=shapes,
        in_specs=[SMEM, HBM],
        out_specs=[VMEM] * len(shapes),
        compiler_params=pltpu.CompilerParams(vmem_limit_bytes=58 * 2**20),
        scratch_shapes=[pltpu.SemaphoreType.DMA((len(plan),))],
        cost_estimate=pl.CostEstimate(flops=0, bytes_accessed=size, transcendentals=0),
    )(ri_order, blocks)


def load(pieces, held, sems, base=0):
    groups = {}
    n = base
    for ref, lead, low, rows, to, at in pieces:
        src = ref if lead is None else ref.at[lead]
        height = src.shape[1]
        for r in range(0, rows, ROWS):
            copy = pltpu.make_async_copy(
                src.at[pl.ds(low + r, ROWS)],
                held.at[pl.ds(to + r, ROWS), pl.ds(at, height)],
                sems.at[n],
            )
            groups.setdefault((to + r) // ROWS, []).append(copy)
            n += 1
    for g in sorted(groups):
        for copy in groups[g]:
            copy.start()
    return groups


def half_step(held, first, occ, vir, keep, mask_t, mix_t, to):
    window = occ.shape[0]
    m = held[first : first + ROWS] * keep[None]
    mask_t[:, to : to + ROWS, :] = jnp.swapaxes(m, 0, 1)
    h = DOT(m.reshape(ROWS * window, window), occ).astype(jnp.bfloat16)
    mixed = [
        DOT(vir, h[p * window : (p + 1) * window]).astype(jnp.bfloat16)[None] for p in range(ROWS)
    ]
    mix_t[:, to : to + ROWS, :] = jnp.swapaxes(jnp.concatenate(mixed), 0, 1)


def front_kernel(places, shifts, outer, orb, count, order_ref, mask_ref, dens_ref, *rest):
    refs = rest[:count]
    mask_t, mix_t, occ_ref, vir_ref, keep_ref, held, sems = rest[count:]
    pieces = [(refs[p[0]],) + p[1:] for p in places]
    groups = load(pieces, held, sems)
    me = lax.axis_index("wide")
    plane, lane = me // PLANE, me % PLANE
    window = occ_ref.shape[0]
    nblk = mask_ref.shape[2]
    block_rows = window // nblk

    def assembled(shape, dim):
        at = lax.broadcasted_iota(jnp.int32, shape, dim)
        place = at // (PLANE * orb)
        device = (at // orb) % PLANE
        source = jnp.zeros(shape, jnp.int32)
        for n, dz in enumerate(shifts):
            who = (device ^ lane) if n == 1 else device
            from_plane = lax.rem(plane + (outer - dz), outer)
            source = jnp.where(place == n, from_plane * PLANE + who, source)
        return source * orb + at % orb

    arrived = lax.broadcasted_iota(jnp.int32, (window, 2 * window), 1)
    kind = (arrived // orb) % 2
    dz = (arrived // (2 * orb)) % outer
    device = arrived // (2 * orb * outer)
    source = lax.rem(plane - dz + outer, outer) * PLANE + device
    orbital = source * orb + arrived % orb
    rows = lax.broadcasted_iota(jnp.int32, (window, 2 * window), 0)
    pick = jnp.where((rows == orbital) & (kind == 0), 1.0, 0.0).astype(jnp.bfloat16)
    dens = dens_ref[...]
    occ = DOT(pick, dens).astype(jnp.bfloat16)
    pick = (assembled((window, 2 * window), 0) == orbital) & (kind == 1)
    pick = jnp.where(pick, 1.0, 0.0).astype(jnp.bfloat16)
    vir = DOT(pick, dens).astype(jnp.bfloat16)
    rows = lax.broadcasted_iota(jnp.int32, (window, window), 0)
    pick = jnp.where(rows == assembled((window, window), 1), 1.0, 0.0).astype(jnp.bfloat16)
    vir = DOT(vir, pick).astype(jnp.bfloat16)
    block = order_ref[me]
    lam = assembled((window, window), 0) // block_rows
    sig = lax.broadcasted_iota(jnp.int32, (window, window), 1) // block_rows
    keep = jnp.zeros((window, window), jnp.int32)
    for a in range(nblk):
        for b in range(nblk):
            keep = jnp.where((lam == a) & (sig == b), mask_ref[block, a, b], keep)
    keep = jnp.where(keep > 0, 1.0, 0.0).astype(jnp.bfloat16)
    occ_ref[...] = occ
    vir_ref[...] = vir
    keep_ref[...] = keep
    for g in sorted(groups):
        for copy in groups[g]:
            copy.wait()
        half_step(held, g * ROWS, occ, vir, keep, mask_t, mix_t, g * ROWS)


def middle_kernel(places, count, occ_ref, vir_ref, keep_ref, *rest):
    refs = rest[:count]
    mask_t, mix_t, held, sems = rest[count:]
    groups = load([(refs[p[0]],) + p[1:] for p in places], held, sems)
    occ, vir, keep = occ_ref[...], vir_ref[...], keep_ref[...]
    for g in sorted(groups):
        for copy in groups[g]:
            copy.wait()
        half_step(held, g * ROWS, occ, vir, keep, mask_t, mix_t, g * ROWS)


def back_kernel(places, count, occ_ref, vir_ref, keep_ref, mask_a, mask_b, mix_a, mix_b, *rest):
    refs = rest[:count]
    out_ref, mask_t, mix_t, held, sems = rest[count:]
    early, done = mask_a.shape[1], mask_a.shape[1] + mask_b.shape[1]
    groups = load([(refs[p[0]],) + p[1:] for p in places], held, sems, 4)
    before = []
    for n, (src, to) in enumerate(
        ((mask_a, mask_t), (mix_a, mix_t), (mask_b, mask_t), (mix_b, mix_t))
    ):
        low = 0 if n < 2 else early
        size = src.shape[1]
        before.append(pltpu.make_async_copy(src, to.at[:, pl.ds(low, size)], sems.at[n]))
    for copy in before:
        copy.start()
    occ, vir, keep = occ_ref[...], vir_ref[...], keep_ref[...]
    for g in sorted(groups):
        for copy in groups[g]:
            copy.wait()
        half_step(held, g * ROWS, occ, vir, keep, mask_t, mix_t, done + g * ROWS)
    for copy in before:
        copy.wait()
    window, rows = mask_t.shape[0], mask_t.shape[1]
    deep = 16

    def body(step, total):
        for k in range(deep):
            m = step * deep + k
            total += lax.dot_general(
                mask_t[m], mix_t[m], (((1,), (1,)), ((), ())), preferred_element_type=jnp.float32
            )
        return total

    total = lax.fori_loop(0, window // deep, body, jnp.zeros((rows, rows), jnp.float32))
    half = rows // 2
    turned = jnp.concatenate([total[half:], total[:half]], axis=0)
    turned = jnp.concatenate([turned[:, half:], turned[:, :half]], axis=1)
    out_ref[...] = jnp.where(lax.axis_index("groups") == 0, total, turned)


def shards(tensor, occupied, virtual, block_mask, ri_order):
    wide_count = lax.axis_size("wide")
    outer = wide_count // PLANE
    ri_total, orb, window = tensor.shape
    rows = ri_total // wide_count
    half = rows // 2
    quarter = half // 2
    kind = tensor.dtype
    barrier = lax.optimization_barrier
    planes = [[PLANE * z + i for i in range(PLANE)] for z in range(outer)]

    def inplane(x):
        return lax.all_to_all(
            x, "wide", split_axis=0, concat_axis=0, tiled=True, axis_index_groups=planes
        )

    def shift(x, dz, flip=0):
        pairs = [
            (w, ((w // PLANE + dz) % outer) * PLANE + ((w % PLANE) ^ flip))
            for w in range(wide_count)
        ]
        return lax.ppermute(x, "wide", pairs)

    def swap(x):
        return lax.ppermute(x, "groups", [(0, 1), (1, 0)])

    order = [d for d in range(1, outer) if d != outer // 2] + [outer // 2]
    first, last = order[0], order[-1]
    shape = lambda *s: jax.ShapeDtypeStruct(s + (orb, window), kind)
    blocks = tensor.reshape(wide_count, rows, orb, window)

    plan = [(q, None, first, q, True, 0, half, True) for q in range(PLANE)]
    pieces = gather(plan, [shape(half)] * PLANE, outer, half, ri_order, blocks)
    base = jnp.stack([occupied, virtual])
    pieces, base = barrier((pieces, base))
    sent = [shift(p, first, q) for q, p in enumerate(pieces)]
    early = shift(base, first)
    held_back, early, base = barrier((blocks, early, base))
    plan, shapes = [], []
    for d in order[1:]:
        plan += [(len(shapes), (i, 0), d, i, False, 0, half, True) for i in range(PLANE)]
        shapes.append(shape(PLANE, half))
    for own in (True, False):
        plan += [(len(shapes), (i, 0), 0, i, False, 0, half, own) for i in range(PLANE)]
        shapes.append(shape(PLANE, half))
    to_send = gather(plan, shapes, outer, half, ri_order, held_back)

    dens, small = {0: base, first: early}, [d for d in range(1, outer) if d != first]
    per_phase = -(-len(small) // max(1, outer - 3))
    own_in, swapped, near = [], [], []
    ready = []
    for k in range(outer):
        if k == 0:
            moved = sent
        elif k <= outer - 3:
            moved = [shift(ready[0], order[k])]
        else:
            moved = [shift(ready[k - outer + 2], last)]
        turn = [swap(own_in[-1])] if k else []
        tiny = []
        if 1 <= k <= outer - 3:
            now, small = small[:per_phase], small[per_phase:]
            tiny = [shift(base, d) for d in now]
        if k == outer - 2:
            spread = jnp.stack([dens[d] for d in range(outer)]).reshape(1, 2 * outer, orb, window)
            spread = jnp.broadcast_to(spread, (PLANE, 2 * outer, orb, window))
            around = inplane(jnp.concatenate([to_send[0], spread], axis=1))
        else:
            around = inplane(to_send[0])
        moved, turn, tiny, around, to_send, base, ready = barrier(
            (moved, turn, tiny, around, to_send[1:], base, ready)
        )
        own_in.append(moved[0] if k else jnp.stack(moved))
        swapped += turn
        dens.update(zip(now, tiny)) if tiny else None
        if k < outer - 3:
            ready = [around]
        elif k == outer - 3:
            ready = [around[:, :quarter], around[:, quarter:]]
        else:
            near.append(around)
    swapped.append(swap(own_in[-1]))
    dens_all = near[0][:, half:].reshape(2 * window, window)

    table = {0: [], 1: [], 2: []}
    for i in range(PLANE):
        for n in range(outer):
            at = (n * PLANE + i) * orb
            if n == 0:
                low, high, low_y, high_y = near[0], near[0], near[1], near[1]
                second, second_y = quarter, quarter
            elif n < outer - 1:
                low, high, low_y, high_y = own_in[n - 1], own_in[n - 1], swapped[n - 1], swapped[n - 1]
                second, second_y = quarter, quarter
            else:
                low, high, low_y, high_y = own_in[-2], own_in[-1], swapped[-2], swapped[-1]
                second, second_y = 0, 0
            table[0] += [(low, i, 0, quarter, 0, at)]
            table[1] += [(high, i, second, quarter, 0, at), (low_y, i, 0, quarter, quarter, at)]
            table[2] += [(high_y, i, second_y, quarter, 0, at)]

    def places(listed):
        if orb % ROWS == 0:
            arrays = []
            for p in listed:
                if not any(p[0] is a for a in arrays):
                    arrays.append(p[0])
            number = lambda x: [x is a for a in arrays].index(True)
            return [(number(p[0]),) + p[1:] for p in listed], arrays
        size = max(p[4] + p[3] for p in listed)
        whole = []
        for r in range(0, size, ROWS):
            row = sorted((p for p in listed if p[4] <= r < p[4] + p[3]), key=lambda p: p[5])
            cut = [lax.slice_in_dim(p[0][p[1]], p[2] + r - p[4], p[2] + r - p[4] + ROWS) for p in row]
            whole.append(jnp.concatenate(cut, axis=1))
        return [(0, None, 0, size, 0, 0)], [jnp.concatenate(whole)]

    def copies(table):
        return sum(p[3] // ROWS for p in table)

    params = pltpu.CompilerParams(vmem_limit_bytes=58 * 2**20)
    mat = jax.ShapeDtypeStruct((window, window), kind)
    tall = lambda n: jax.ShapeDtypeStruct((window, n, window), kind)

    def cost(n, moved):
        return pl.CostEstimate(
            flops=4 * n * window**3, bytes_accessed=moved * window**2, transcendentals=0
        )

    def scratch(n, extra):
        return [
            pltpu.VMEM((n, window, window), kind),
            pltpu.SemaphoreType.DMA((extra,)),
        ]

    rows_of, arrays = places(table[0])
    mask_a, mix_a, occ, vir, keep = pl.pallas_call(
        functools.partial(front_kernel, rows_of, [0] + order, outer, orb, len(arrays)),
        out_shape=[tall(quarter), tall(quarter), mat, mat, mat],
        in_specs=[SMEM, SMEM, VMEM] + [HBM] * len(arrays),
        out_specs=[VMEM] * 5,
        scratch_shapes=scratch(quarter, copies(rows_of)),
        compiler_params=params,
        cost_estimate=cost(quarter, 6 * quarter),
    )(ri_order, block_mask, dens_all, *arrays)
    rows_of, arrays = places(table[1])
    mask_b, mix_b = pl.pallas_call(
        functools.partial(middle_kernel, rows_of, len(arrays)),
        out_shape=[tall(half), tall(half)],
        in_specs=[VMEM] * 3 + [HBM] * len(arrays),
        out_specs=[VMEM] * 2,
        scratch_shapes=scratch(half, copies(rows_of)),
        compiler_params=params,
        cost_estimate=cost(half, 6 * half),
    )(occ, vir, keep, *arrays)
    rows_of, arrays = places(table[2])
    return pl.pallas_call(
        functools.partial(back_kernel, rows_of, len(arrays)),
        out_shape=jax.ShapeDtypeStruct((rows, rows), jnp.float32),
        in_specs=[VMEM] * 3 + [HBM] * (4 + len(arrays)),
        out_specs=VMEM,
        scratch_shapes=[
            pltpu.VMEM((window, rows, window), kind),
            pltpu.VMEM((window, rows, window), kind),
        ]
        + scratch(quarter, 4 + copies(rows_of)),
        compiler_params=params,
        cost_estimate=cost(quarter, 4 * rows),
    )(occ, vir, keep, mask_a, mask_b, mix_a, mix_b, *arrays)


def solution(mesh):
    in_specs = (
        P(None, "wide", None),
        P(("groups", "wide"), None),
        P(("groups", "wide"), None),
        P(),
        P(),
    )
    out_specs = P(("groups", "wide"), None)
    return jax.shard_map(shards, mesh=mesh, in_specs=in_specs, out_specs=out_specs, check_vma=False)
```

```python
import functools

import jax
import jax.numpy as jnp
from jax import lax
from jax.experimental import pallas as pl
from jax.experimental.pallas import tpu as pltpu
from jax.sharding import PartitionSpec as P

PLANE = 4
WINDOW = 2
ROWS = 16
VMEM = pl.BlockSpec(memory_space=pltpu.VMEM)
SMEM = pl.BlockSpec(memory_space=pltpu.SMEM)
HBM = pl.BlockSpec(memory_space=pl.ANY)
DOT = functools.partial(jnp.dot, preferred_element_type=jnp.float32)


def gather_kernel(plan, tails, outer, half, count, order_ref, blocks_ref, occ_ref, vir_ref, *rest):
    outs, sems = rest[:count], rest[count]
    me = lax.axis_index("wide")
    group = lax.axis_index("groups")
    plane, lane = me // PLANE, me % PLANE
    copies = []
    for n, (out, entry, row, dz, target, flip, start, rows, own) in enumerate(plan):
        who = (lane ^ target) if flip else target
        block = order_ref[lax.rem(plane + dz, outer) * PLANE + who]
        low = (group if own else 1 - group) * half + start
        to = outs[out] if entry is None else outs[out].at[entry]
        copies.append(
            pltpu.make_async_copy(
                blocks_ref.at[block, pl.ds(low, rows)], to.at[pl.ds(row, rows)], sems.at[n]
            )
        )
    for n, (out, row) in enumerate(tails):
        for m, part in enumerate((occ_ref, vir_ref)):
            to = outs[out].at[row + m]
            copies.append(pltpu.make_async_copy(part, to, sems.at[len(plan) + 2 * n + m]))
    for copy in copies:
        copy.start()
    for copy in copies:
        copy.wait()


def gather(plan, tails, shapes, outer, half, ri_order, blocks, occupied, virtual):
    size = sum(s.size for s in shapes) * 4
    return pl.pallas_call(
        functools.partial(gather_kernel, plan, tails, outer, half, len(shapes)),
        out_shape=shapes,
        in_specs=[SMEM] + [HBM] * 3,
        out_specs=[VMEM] * len(shapes),
        compiler_params=pltpu.CompilerParams(vmem_limit_bytes=58 * 2**20),
        scratch_shapes=[pltpu.SemaphoreType.DMA((len(plan) + 2 * len(tails),))],
        cost_estimate=pl.CostEstimate(flops=0, bytes_accessed=size, transcendentals=0),
    )(ri_order, blocks, occupied, virtual)


def load(pieces, held, sems, base=0):
    groups = {}
    n = base
    for ref, lead, low, rows, to, at in pieces:
        src = ref if lead is None else ref.at[lead]
        height = src.shape[1]
        for r in range(0, rows, ROWS):
            copy = pltpu.make_async_copy(
                src.at[pl.ds(low + r, ROWS)],
                held.at[pl.ds(to + r, ROWS), pl.ds(at, height)],
                sems.at[n],
            )
            groups.setdefault((to + r) // ROWS, []).append(copy)
            n += 1
    for g in sorted(groups):
        for copy in groups[g]:
            copy.start()
    return groups


def half_step(held, first, occ, vir, keep, mask_t, mix_t, to):
    window = occ.shape[0]
    m = held[first : first + ROWS] * keep[None]
    mask_t[:, to : to + ROWS, :] = jnp.swapaxes(m, 0, 1)
    h = DOT(m.reshape(ROWS * window, window), occ).astype(jnp.bfloat16)
    mixed = [
        DOT(vir, h[p * window : (p + 1) * window]).astype(jnp.bfloat16)[None] for p in range(ROWS)
    ]
    mix_t[:, to : to + ROWS, :] = jnp.swapaxes(jnp.concatenate(mixed), 0, 1)


def front_kernel(places, shifts, outer, orb, count, order_ref, mask_ref, dens_ref, *rest):
    refs = rest[:count]
    mask_t, mix_t, occ_ref, vir_ref, keep_ref, held, sems = rest[count:]
    pieces = [(refs[p[0]],) + p[1:] for p in places]
    groups = load(pieces, held, sems)
    me = lax.axis_index("wide")
    plane, lane = me // PLANE, me % PLANE
    window = occ_ref.shape[0]
    nblk = mask_ref.shape[0]
    block_rows = window // nblk

    def assembled(shape, dim):
        at = lax.broadcasted_iota(jnp.int32, shape, dim)
        place = at // (PLANE * orb)
        device = (at // orb) % PLANE
        source = jnp.zeros(shape, jnp.int32)
        for n, dz in enumerate(shifts):
            who = device if n == outer - 1 else device ^ lane
            from_plane = lax.rem(plane + (outer - dz), outer)
            source = jnp.where(place == n, from_plane * PLANE + who, source)
        return source * orb + at % orb

    arrived = lax.broadcasted_iota(jnp.int32, (window, 2 * window), 1)
    kind = (arrived // orb) % 2
    place = (arrived // (2 * orb)) % outer
    device = (arrived // (2 * orb * outer)) ^ lane
    source = jnp.zeros(arrived.shape, jnp.int32)
    for n, dz in enumerate(shifts):
        from_plane = lax.rem(plane + (outer - dz), outer)
        source = jnp.where(place == n, from_plane * PLANE + device, source)
    orbital = source * orb + arrived % orb
    rows = lax.broadcasted_iota(jnp.int32, (window, 2 * window), 0)
    pick = jnp.where((rows == orbital) & (kind == 0), 1.0, 0.0).astype(jnp.bfloat16)
    dens = dens_ref[...]
    occ = DOT(pick, dens).astype(jnp.bfloat16)
    pick = (assembled((window, 2 * window), 0) == orbital) & (kind == 1)
    pick = jnp.where(pick, 1.0, 0.0).astype(jnp.bfloat16)
    vir = DOT(pick, dens).astype(jnp.bfloat16)
    rows = lax.broadcasted_iota(jnp.int32, (window, window), 0)
    pick = jnp.where(rows == assembled((window, window), 1), 1.0, 0.0).astype(jnp.bfloat16)
    vir = DOT(vir, pick).astype(jnp.bfloat16)
    block = order_ref[me]
    lam = assembled((window, window), 0) // block_rows
    sig = lax.broadcasted_iota(jnp.int32, (window, window), 1) // block_rows
    keep = jnp.zeros((window, window), jnp.int32)
    for a in range(nblk):
        for b in range(nblk):
            keep = jnp.where((lam == a) & (sig == b), mask_ref[a, b, block], keep)
    keep = jnp.where(keep > 0, 1.0, 0.0).astype(jnp.bfloat16)
    occ_ref[...] = occ
    vir_ref[...] = vir
    keep_ref[...] = keep
    for g in sorted(groups):
        for copy in groups[g]:
            copy.wait()
        half_step(held, g * ROWS, occ, vir, keep, mask_t, mix_t, g * ROWS)


def middle_kernel(places, count, occ_ref, vir_ref, keep_ref, *rest):
    refs = rest[:count]
    mask_t, mix_t, held, sems = rest[count:]
    groups = load([(refs[p[0]],) + p[1:] for p in places], held, sems)
    occ, vir, keep = occ_ref[...], vir_ref[...], keep_ref[...]
    for g in sorted(groups):
        for copy in groups[g]:
            copy.wait()
        half_step(held, g * ROWS, occ, vir, keep, mask_t, mix_t, g * ROWS)


def back_kernel(places, count, occ_ref, vir_ref, keep_ref, mask_a, mask_b, mix_a, mix_b, *rest):
    refs = rest[:count]
    out_ref, mask_t, mix_t, held, sems = rest[count:]
    early, done = mask_a.shape[1], mask_a.shape[1] + mask_b.shape[1]
    groups = load([(refs[p[0]],) + p[1:] for p in places], held, sems, 4)
    before = []
    for n, (src, to) in enumerate(
        ((mask_a, mask_t), (mix_a, mix_t), (mask_b, mask_t), (mix_b, mix_t))
    ):
        low = 0 if n < 2 else early
        size = src.shape[1]
        before.append(pltpu.make_async_copy(src, to.at[:, pl.ds(low, size)], sems.at[n]))
    for copy in before:
        copy.start()
    occ, vir, keep = occ_ref[...], vir_ref[...], keep_ref[...]
    for g in sorted(groups):
        for copy in groups[g]:
            copy.wait()
        half_step(held, g * ROWS, occ, vir, keep, mask_t, mix_t, done + g * ROWS)
    for copy in before:
        copy.wait()
    window, rows = mask_t.shape[0], mask_t.shape[1]
    deep = 16

    def body(step, total):
        for k in range(deep):
            m = step * deep + k
            total += lax.dot_general(
                mask_t[m], mix_t[m], (((1,), (1,)), ((), ())), preferred_element_type=jnp.float32
            )
        return total

    total = lax.fori_loop(0, window // deep, body, jnp.zeros((rows, rows), jnp.float32))
    half = rows // 2
    turned = jnp.concatenate([total[half:], total[:half]], axis=0)
    turned = jnp.concatenate([turned[:, half:], turned[:, :half]], axis=1)
    out_ref[...] = jnp.where(lax.axis_index("groups") == 0, total, turned)


def shards(tensor, occupied, virtual, block_mask, ri_order):
    wide_count = lax.axis_size("wide")
    outer = wide_count // PLANE
    ri_total, orb, window = tensor.shape
    rows = ri_total // wide_count
    half = rows // 2
    quarter = half // 2
    kind = tensor.dtype
    barrier = lax.optimization_barrier
    planes = [[PLANE * z + i for i in range(PLANE)] for z in range(outer)]

    def inplane(x):
        return lax.all_to_all(
            x, "wide", split_axis=0, concat_axis=0, tiled=True, axis_index_groups=planes
        )

    def shift(x, dz, flip=0):
        pairs = [
            (w, ((w // PLANE + dz) % outer) * PLANE + ((w % PLANE) ^ flip))
            for w in range(wide_count)
        ]
        return lax.ppermute(x, "wide", pairs)

    def swap(x):
        return lax.ppermute(x, "groups", [(0, 1), (1, 0)])

    order = [d for d in range(1, outer) if d != outer // 2] + [outer // 2]
    first, last = order[0], order[-1]
    shape = lambda *s: jax.ShapeDtypeStruct(s + (orb, window), kind)
    blocks = tensor.reshape(wide_count, rows, orb, window)

    def straight(d, at):
        plan = [(at + q, None, 0, d, q, True, 0, half, True) for q in range(PLANE)]
        return plan, [(at, half)], [shape(half + 2)] + [shape(half)] * (PLANE - 1)

    plan, tails, shapes = straight(first, 0)
    pieces = gather(plan, tails, shapes, outer, half, ri_order, blocks, occupied, virtual)
    pieces, held_back = barrier((pieces, blocks))
    plan, tails, shapes = [], [], []
    for d in order[1:-1]:
        more = straight(d, len(shapes))
        plan, tails, shapes = plan + more[0], tails + more[1], shapes + more[2]
    plan += [(len(shapes), i, 0, last, i, False, 0, half, True) for i in range(PLANE)]
    shapes.append(shape(PLANE, half))
    for q in range(PLANE):
        plan += [(len(shapes), None, 0, 0, q, True, 0, half, True)]
        plan += [(len(shapes), None, half, 0, q, True, 0, half, False)]
        shapes.append(shape(rows))
    to_send = gather(plan, tails, shapes, outer, half, ri_order, held_back, occupied, virtual)

    def after(x, other):
        return barrier((x, other))[0]

    direct = list(pieces) + list(to_send[: PLANE * (outer - 3)])
    to_last, near_out = to_send[PLANE * (outer - 3)], to_send[PLANE * (outer - 3) + 1 :]
    base = jnp.stack([occupied, virtual])
    far = shift(base, last)
    came, swapped = [], []
    for n, piece in enumerate(direct):
        if n >= WINDOW:
            piece = after(piece, came[n - WINDOW])
        came.append(shift(piece, order[n // PLANE], n % PLANE))
    ready = inplane(after(to_last, came[1]))
    low = shift(after(ready[:, :quarter], came[-2]), last)
    high = shift(after(ready[:, quarter:], came[-1]), last)
    for n in range(outer - 2):
        group_in = came[PLANE * n : PLANE * (n + 1)]
        swapped.append(swap(jnp.stack([group_in[0][:half]] + group_in[1:])))
    near = [near_out[0]]
    for q in range(1, PLANE):
        near.append(shift(after(near_out[q], near[-1] if q > 1 else came[-PLANE]), 0, q))
    mine = jnp.stack([base] + [came[PLANE * n][half:] for n in range(outer - 2)] + [far])
    dens = [mine] + [shift(mine, 0, q) for q in range(1, PLANE)]
    dens_all = jnp.stack(dens).reshape(2 * window, window)
    swapped.append(swap(low))

    early, front, back = [], [], []
    for i in range(PLANE):
        for n in range(outer):
            at = (n * PLANE + i) * orb
            if n == 0:
                early += [(near[i], None, 0, quarter, 0, at)]
                front += [(near[i], None, quarter, half, 0, at)]
                back += [(near[i], None, half + quarter, quarter, 0, at)]
            elif n < outer - 1:
                early += [(came[PLANE * (n - 1) + i], None, 0, quarter, 0, at)]
                front += [(came[PLANE * (n - 1) + i], None, quarter, quarter, 0, at)]
                front += [(swapped[n - 1], i, 0, quarter, quarter, at)]
                back += [(swapped[n - 1], i, quarter, quarter, 0, at)]
            else:
                early += [(low, i, 0, quarter, 0, at)]
                front += [(high, i, 0, quarter, 0, at)]
                front += [(swapped[-1], i, 0, quarter, quarter, at)]

    def places(listed):
        if orb % ROWS == 0:
            arrays = []
            for p in listed:
                if not any(p[0] is a for a in arrays):
                    arrays.append(p[0])
            number = lambda x: [x is a for a in arrays].index(True)
            return [(number(p[0]),) + p[1:] for p in listed], arrays
        size = max(p[4] + p[3] for p in listed)
        whole = []
        for r in range(0, size, ROWS):
            row = sorted((p for p in listed if p[4] <= r < p[4] + p[3]), key=lambda p: p[5])
            cut = [lax.slice_in_dim(p[0] if p[1] is None else p[0][p[1]], p[2] + r - p[4], p[2] + r - p[4] + ROWS) for p in row]
            whole.append(jnp.concatenate(cut, axis=1))
        return [(0, None, 0, size, 0, 0)], [jnp.concatenate(whole)]

    def copies(table):
        return sum(p[3] // ROWS for p in table)

    params = pltpu.CompilerParams(vmem_limit_bytes=58 * 2**20)
    mat = jax.ShapeDtypeStruct((window, window), kind)
    tall = lambda n: jax.ShapeDtypeStruct((window, n, window), kind)

    def cost(n, moved):
        return pl.CostEstimate(
            flops=4 * n * window**3, bytes_accessed=moved * window**2, transcendentals=0
        )

    def scratch(n, extra):
        return [
            pltpu.VMEM((n, window, window), kind),
            pltpu.SemaphoreType.DMA((extra,)),
        ]

    rows_of, arrays = places(early)
    mask_a, mix_a, occ, vir, keep = pl.pallas_call(
        functools.partial(front_kernel, rows_of, [0] + order, outer, orb, len(arrays)),
        out_shape=[tall(quarter), tall(quarter), mat, mat, mat],
        in_specs=[SMEM, SMEM, VMEM] + [HBM] * len(arrays),
        out_specs=[VMEM] * 5,
        scratch_shapes=scratch(quarter, copies(rows_of)),
        compiler_params=params,
        cost_estimate=cost(quarter, 6 * quarter),
    )(ri_order, block_mask.transpose(1, 2, 0), dens_all, *arrays)
    final = swap(after(high, mask_a))
    back += [(final, i, 0, quarter, 0, ((outer - 1) * PLANE + i) * orb) for i in range(PLANE)]
    rows_of, arrays = places(front)
    mask_b, mix_b = pl.pallas_call(
        functools.partial(middle_kernel, rows_of, len(arrays)),
        out_shape=[tall(half), tall(half)],
        in_specs=[VMEM] * 3 + [HBM] * len(arrays),
        out_specs=[VMEM] * 2,
        scratch_shapes=scratch(half, copies(rows_of)),
        compiler_params=params,
        cost_estimate=cost(half, 6 * half),
    )(occ, vir, keep, *arrays)
    rows_of, arrays = places(back)
    return pl.pallas_call(
        functools.partial(back_kernel, rows_of, len(arrays)),
        out_shape=jax.ShapeDtypeStruct((rows, rows), jnp.float32),
        in_specs=[VMEM] * 3 + [HBM] * (4 + len(arrays)),
        out_specs=VMEM,
        scratch_shapes=[
            pltpu.VMEM((window, rows, window), kind),
            pltpu.VMEM((window, rows, window), kind),
        ]
        + scratch(quarter, 4 + copies(rows_of)),
        compiler_params=params,
        cost_estimate=cost(quarter, 4 * rows),
    )(occ, vir, keep, mask_a, mask_b, mix_a, mix_b, *arrays)


def solution(mesh):
    in_specs = (
        P(None, "wide", None),
        P(("groups", "wide"), None),
        P(("groups", "wide"), None),
        P(),
        P(),
    )
    out_specs = P(("groups", "wide"), None)
    return jax.shard_map(shards, mesh=mesh, in_specs=in_specs, out_specs=out_specs, check_vma=False)
```

```python
import functools

import jax
import jax.numpy as jnp
from jax import lax
from jax.experimental import pallas as pl
from jax.experimental.pallas import tpu as pltpu
from jax.sharding import PartitionSpec as P

PLANE = 4
WINDOW = 2
LIM = (16, 24, 28)
CHUNKS = 4
ROWS = 16
VMEM = pl.BlockSpec(memory_space=pltpu.VMEM)
SMEM = pl.BlockSpec(memory_space=pltpu.SMEM)
HBM = pl.BlockSpec(memory_space=pl.ANY)
DOT = functools.partial(jnp.dot, preferred_element_type=jnp.float32)


def gather_kernel(plan, tails, outer, half, count, order_ref, blocks_ref, occ_ref, vir_ref, *rest):
    outs, sems = rest[:count], rest[count]
    me = lax.axis_index("wide")
    group = lax.axis_index("groups")
    plane, lane = me // PLANE, me % PLANE
    copies = []
    for n, (out, entry, row, dz, target, flip, start, rows, own) in enumerate(plan):
        who = (lane ^ target) if flip else target
        block = order_ref[lax.rem(plane + dz, outer) * PLANE + who]
        low = (group if own else 1 - group) * half + start
        to = outs[out] if entry is None else outs[out].at[entry]
        copies.append(
            pltpu.make_async_copy(
                blocks_ref.at[block, pl.ds(low, rows)], to.at[pl.ds(row, rows)], sems.at[n]
            )
        )
    for n, (out, row) in enumerate(tails):
        for m, part in enumerate((occ_ref, vir_ref)):
            to = outs[out].at[row + m]
            copies.append(pltpu.make_async_copy(part, to, sems.at[len(plan) + 2 * n + m]))
    for copy in copies:
        copy.start()
    for copy in copies:
        copy.wait()


def gather(plan, tails, shapes, outer, half, ri_order, blocks, occupied, virtual):
    size = sum(s.size for s in shapes) * 4
    return pl.pallas_call(
        functools.partial(gather_kernel, plan, tails, outer, half, len(shapes)),
        out_shape=shapes,
        in_specs=[SMEM] + [HBM] * 3,
        out_specs=[VMEM] * len(shapes),
        compiler_params=pltpu.CompilerParams(vmem_limit_bytes=58 * 2**20),
        scratch_shapes=[pltpu.SemaphoreType.DMA((len(plan) + 2 * len(tails),))],
        cost_estimate=pl.CostEstimate(flops=0, bytes_accessed=size, transcendentals=0),
    )(ri_order, blocks, occupied, virtual)


def load(pieces, held, sems, base=0):
    groups = {}
    n = base
    for ref, lead, low, rows, to, at in pieces:
        src = ref if lead is None else ref.at[lead]
        height = src.shape[1]
        for r in range(0, rows, ROWS):
            copy = pltpu.make_async_copy(
                src.at[pl.ds(low + r, ROWS)],
                held.at[pl.ds(to + r, ROWS), pl.ds(at, height)],
                sems.at[n],
            )
            groups.setdefault((to + r) // ROWS, []).append(copy)
            n += 1
    for g in sorted(groups):
        for copy in groups[g]:
            copy.start()
    return groups


def half_step(held, first, occ, vir, keep, mask_t, mix_t, to):
    window = occ.shape[0]
    m = held[first : first + ROWS] * keep[None]
    mask_t[:, to : to + ROWS, :] = jnp.swapaxes(m, 0, 1)
    h = DOT(m.reshape(ROWS * window, window), occ).astype(jnp.bfloat16)
    mixed = [
        DOT(vir, h[p * window : (p + 1) * window]).astype(jnp.bfloat16)[None] for p in range(ROWS)
    ]
    mix_t[:, to : to + ROWS, :] = jnp.swapaxes(jnp.concatenate(mixed), 0, 1)


def front_kernel(places, shifts, outer, orb, count, order_ref, mask_ref, dens_ref, *rest):
    refs = rest[:count]
    mask_t, mix_t, occ_ref, vir_ref, keep_ref, held, sems = rest[count:]
    pieces = [(refs[p[0]],) + p[1:] for p in places]
    groups = load(pieces, held, sems)
    me = lax.axis_index("wide")
    plane, lane = me // PLANE, me % PLANE
    window = occ_ref.shape[0]
    nblk = mask_ref.shape[0]
    block_rows = window // nblk

    def assembled(shape, dim):
        at = lax.broadcasted_iota(jnp.int32, shape, dim)
        place = at // (PLANE * orb)
        device = (at // orb) % PLANE
        source = jnp.zeros(shape, jnp.int32)
        for n, dz in enumerate(shifts):
            who = device if n == outer - 1 else device ^ lane
            from_plane = lax.rem(plane + (outer - dz), outer)
            source = jnp.where(place == n, from_plane * PLANE + who, source)
        return source * orb + at % orb

    arrived = lax.broadcasted_iota(jnp.int32, (window, 2 * window), 1)
    kind = (arrived // orb) % 2
    place = (arrived // (2 * orb)) % outer
    device = (arrived // (2 * orb * outer)) ^ lane
    source = jnp.zeros(arrived.shape, jnp.int32)
    for n, dz in enumerate(shifts):
        from_plane = lax.rem(plane + (outer - dz), outer)
        source = jnp.where(place == n, from_plane * PLANE + device, source)
    orbital = source * orb + arrived % orb
    rows = lax.broadcasted_iota(jnp.int32, (window, 2 * window), 0)
    pick = jnp.where((rows == orbital) & (kind == 0), 1.0, 0.0).astype(jnp.bfloat16)
    dens = dens_ref[...]
    occ = DOT(pick, dens).astype(jnp.bfloat16)
    pick = (assembled((window, 2 * window), 0) == orbital) & (kind == 1)
    pick = jnp.where(pick, 1.0, 0.0).astype(jnp.bfloat16)
    vir = DOT(pick, dens).astype(jnp.bfloat16)
    rows = lax.broadcasted_iota(jnp.int32, (window, window), 0)
    pick = jnp.where(rows == assembled((window, window), 1), 1.0, 0.0).astype(jnp.bfloat16)
    vir = DOT(vir, pick).astype(jnp.bfloat16)
    block = order_ref[me]
    lam = assembled((window, window), 0) // block_rows
    sig = lax.broadcasted_iota(jnp.int32, (window, window), 1) // block_rows
    keep = jnp.zeros((window, window), jnp.int32)
    for a in range(nblk):
        for b in range(nblk):
            keep = jnp.where((lam == a) & (sig == b), mask_ref[a, b, block], keep)
    keep = jnp.where(keep > 0, 1.0, 0.0).astype(jnp.bfloat16)
    occ_ref[...] = occ
    vir_ref[...] = vir
    keep_ref[...] = keep
    for g in sorted(groups):
        for copy in groups[g]:
            copy.wait()
        half_step(held, g * ROWS, occ, vir, keep, mask_t, mix_t, g * ROWS)


def middle_kernel(places, count, occ_ref, vir_ref, keep_ref, *rest):
    refs = rest[:count]
    mask_t, mix_t, held, sems = rest[count:]
    groups = load([(refs[p[0]],) + p[1:] for p in places], held, sems)
    occ, vir, keep = occ_ref[...], vir_ref[...], keep_ref[...]
    for g in sorted(groups):
        for copy in groups[g]:
            copy.wait()
        half_step(held, g * ROWS, occ, vir, keep, mask_t, mix_t, g * ROWS)


def back_kernel(places, count, occ_ref, vir_ref, keep_ref, mask_a, mask_b, mix_a, mix_b, *rest):
    refs = rest[:count]
    out_ref, mask_c, mix_c, held, sems = rest[count:]
    groups = load([(refs[p[0]],) + p[1:] for p in places], held, sems)
    occ, vir, keep = occ_ref[...], vir_ref[...], keep_ref[...]
    for g in sorted(groups):
        for copy in groups[g]:
            copy.wait()
        half_step(held, g * ROWS, occ, vir, keep, mask_c, mix_c, g * ROWS)
    window, rows = mask_c.shape[0], out_ref.shape[0]
    deep = window // CHUNKS

    def body(step, total):
        for k in range(deep):
            m = step * deep + k
            left = jnp.concatenate([mask_a[m], mask_b[m], mask_c[m]])
            right = jnp.concatenate([mix_a[m], mix_b[m], mix_c[m]])
            total += lax.dot_general(
                left, right, (((1,), (1,)), ((), ())), preferred_element_type=jnp.float32
            )
        return total

    total = lax.fori_loop(0, CHUNKS, body, jnp.zeros((rows, rows), jnp.float32))
    half = rows // 2
    turned = jnp.concatenate([total[half:], total[:half]], axis=0)
    turned = jnp.concatenate([turned[:, half:], turned[:, :half]], axis=1)
    out_ref[...] = jnp.where(lax.axis_index("groups") == 0, total, turned)


def shards(tensor, occupied, virtual, block_mask, ri_order):
    wide_count = lax.axis_size("wide")
    outer = wide_count // PLANE
    ri_total, orb, window = tensor.shape
    rows = ri_total // wide_count
    half = rows // 2
    quarter = half // 2
    kind = tensor.dtype
    barrier = lax.optimization_barrier
    planes = [[PLANE * z + i for i in range(PLANE)] for z in range(outer)]

    def inplane(x):
        return lax.all_to_all(
            x, "wide", split_axis=0, concat_axis=0, tiled=True, axis_index_groups=planes
        )

    def shift(x, dz, flip=0):
        pairs = [
            (w, ((w // PLANE + dz) % outer) * PLANE + ((w % PLANE) ^ flip))
            for w in range(wide_count)
        ]
        return lax.ppermute(x, "wide", pairs)

    def swap(x):
        return lax.ppermute(x, "groups", [(0, 1), (1, 0)])

    order = [d for d in range(1, outer) if d != outer // 2] + [outer // 2]
    first, last = order[0], order[-1]
    shape = lambda *s: jax.ShapeDtypeStruct(s + (orb, window), kind)
    blocks = tensor.reshape(wide_count, rows, orb, window)

    def straight(d, at):
        plan = [(at + q, None, 0, d, q, True, 0, half, True) for q in range(PLANE)]
        return plan, [(at, half)], [shape(half + 2)] + [shape(half)] * (PLANE - 1)

    plan, tails, shapes = straight(first, 0)
    pieces = gather(plan, tails, shapes, outer, half, ri_order, blocks, occupied, virtual)
    pieces, held_back = barrier((pieces, blocks))
    plan, tails, shapes = [], [], []
    for d in order[1:-1]:
        more = straight(d, len(shapes))
        plan, tails, shapes = plan + more[0], tails + more[1], shapes + more[2]
    plan += [(len(shapes), i, 0, last, i, False, 0, half, True) for i in range(PLANE)]
    shapes.append(shape(PLANE, half))
    for q in range(PLANE):
        plan += [(len(shapes), None, 0, 0, q, True, 0, half, True)]
        plan += [(len(shapes), None, half, 0, q, True, 0, half, False)]
        shapes.append(shape(rows))
    to_send = gather(plan, tails, shapes, outer, half, ri_order, held_back, occupied, virtual)

    def after(x, other):
        return barrier((x, other))[0]

    direct = list(pieces) + list(to_send[: PLANE * (outer - 3)])
    to_last, near_out = to_send[PLANE * (outer - 3)], to_send[PLANE * (outer - 3) + 1 :]
    base = jnp.stack([occupied, virtual])
    far = shift(base, last)
    came, swapped = [], []
    for n, piece in enumerate(direct):
        if n >= WINDOW:
            piece = after(piece, came[n - WINDOW])
        came.append(shift(piece, order[n // PLANE], n % PLANE))
    ready = inplane(after(to_last, came[1]))
    low = shift(after(ready[:, :quarter], came[-2]), last)
    high = shift(after(ready[:, quarter:], came[-1]), last)
    for n in range(outer - 2):
        group_in = came[PLANE * n : PLANE * (n + 1)]
        swapped.append(swap(jnp.stack([group_in[0][:half]] + group_in[1:])))
    near = [near_out[0]]
    for q in range(1, PLANE):
        near.append(shift(after(near_out[q], near[-1] if q > 1 else came[-PLANE]), 0, q))
    mine = jnp.stack([base] + [came[PLANE * n][half:] for n in range(outer - 2)] + [far])
    dens = [mine] + [shift(mine, 0, q) for q in range(1, PLANE)]
    dens_all = jnp.stack(dens).reshape(2 * window, window)
    swapped.append(swap(low))

    early, front, back = [], [], []
    for i in range(PLANE):
        for n in range(outer):
            at = (n * PLANE + i) * orb
            if n == 0:
                early += [(near[i], None, 0, quarter, 0, at)]
                front += [(near[i], None, quarter, half, 0, at)]
                back += [(near[i], None, half + quarter, quarter, 0, at)]
            elif n < outer - 1:
                early += [(came[PLANE * (n - 1) + i], None, 0, quarter, 0, at)]
                front += [(came[PLANE * (n - 1) + i], None, quarter, quarter, 0, at)]
                front += [(swapped[n - 1], i, 0, quarter, quarter, at)]
                back += [(swapped[n - 1], i, quarter, quarter, 0, at)]
            else:
                early += [(low, i, 0, quarter, 0, at)]
                front += [(high, i, 0, quarter, 0, at)]
                front += [(swapped[-1], i, 0, quarter, quarter, at)]

    def places(listed):
        if orb % ROWS == 0:
            arrays = []
            for p in listed:
                if not any(p[0] is a for a in arrays):
                    arrays.append(p[0])
            number = lambda x: [x is a for a in arrays].index(True)
            return [(number(p[0]),) + p[1:] for p in listed], arrays
        size = max(p[4] + p[3] for p in listed)
        whole = []
        for r in range(0, size, ROWS):
            row = sorted((p for p in listed if p[4] <= r < p[4] + p[3]), key=lambda p: p[5])
            cut = [lax.slice_in_dim(p[0] if p[1] is None else p[0][p[1]], p[2] + r - p[4], p[2] + r - p[4] + ROWS) for p in row]
            whole.append(jnp.concatenate(cut, axis=1))
        return [(0, None, 0, size, 0, 0)], [jnp.concatenate(whole)]

    def copies(table):
        return sum(p[3] // ROWS for p in table)

    params = lambda m: pltpu.CompilerParams(vmem_limit_bytes=m * 2**20)
    mat = jax.ShapeDtypeStruct((window, window), kind)
    tall = lambda n: jax.ShapeDtypeStruct((window, n, window), kind)

    def cost(n, moved):
        return pl.CostEstimate(
            flops=4 * n * window**3, bytes_accessed=moved * window**2, transcendentals=0
        )

    def scratch(n, extra):
        return [
            pltpu.VMEM((n, window, window), kind),
            pltpu.SemaphoreType.DMA((extra,)),
        ]

    rows_of, arrays = places(early)
    mask_a, mix_a, occ, vir, keep = pl.pallas_call(
        functools.partial(front_kernel, rows_of, [0] + order, outer, orb, len(arrays)),
        out_shape=[tall(quarter), tall(quarter), mat, mat, mat],
        in_specs=[SMEM, SMEM, VMEM] + [HBM] * len(arrays),
        out_specs=[VMEM] * 5,
        scratch_shapes=scratch(quarter, copies(rows_of)),
        compiler_params=params(LIM[0]),
        cost_estimate=cost(quarter, 6 * quarter),
    )(ri_order, block_mask.transpose(1, 2, 0), dens_all, *arrays)
    final = swap(after(high, mask_a))
    back += [(final, i, 0, quarter, 0, ((outer - 1) * PLANE + i) * orb) for i in range(PLANE)]
    rows_of, arrays = places(front)
    mask_b, mix_b = pl.pallas_call(
        functools.partial(middle_kernel, rows_of, len(arrays)),
        out_shape=[tall(half), tall(half)],
        in_specs=[VMEM] * 3 + [HBM] * len(arrays),
        out_specs=[VMEM] * 2,
        scratch_shapes=scratch(half, copies(rows_of)),
        compiler_params=params(LIM[1]),
        cost_estimate=cost(half, 6 * half),
    )(occ, vir, keep, *arrays)
    rows_of, arrays = places(back)
    return pl.pallas_call(
        functools.partial(back_kernel, rows_of, len(arrays)),
        out_shape=jax.ShapeDtypeStruct((rows, rows), jnp.float32),
        in_specs=[VMEM] * 7 + [HBM] * len(arrays),
        out_specs=VMEM,
        scratch_shapes=[pltpu.VMEM((window, quarter, window), kind)] * 2
        + scratch(quarter, copies(rows_of)),
        compiler_params=params(LIM[2]),
        cost_estimate=cost(quarter, 4 * rows),
    )(occ, vir, keep, mask_a, mask_b, mix_a, mix_b, *arrays)


def solution(mesh):
    in_specs = (
        P(None, "wide", None),
        P(("groups", "wide"), None),
        P(("groups", "wide"), None),
        P(),
        P(),
    )
    out_specs = P(("groups", "wide"), None)
    return jax.shard_map(shards, mesh=mesh, in_specs=in_specs, out_specs=out_specs, check_vma=False)
```

```python
import functools

import jax
import jax.numpy as jnp
from jax import lax
from jax.experimental import pallas as pl
from jax.experimental.pallas import tpu as pltpu
from jax.sharding import PartitionSpec as P

PLANE = 4
WINDOW = 2
LIM = (16, 24, 28)
CHUNKS = 4
ROWS = 16
VMEM = pl.BlockSpec(memory_space=pltpu.VMEM)
SMEM = pl.BlockSpec(memory_space=pltpu.SMEM)
HBM = pl.BlockSpec(memory_space=pl.ANY)
DOT = functools.partial(jnp.dot, preferred_element_type=jnp.float32)


def gather_kernel(plan, tails, outer, half, count, order_ref, blocks_ref, occ_ref, vir_ref, *rest):
    outs, sems = rest[:count], rest[count]
    me = lax.axis_index("wide")
    group = lax.axis_index("groups")
    plane, lane = me // PLANE, me % PLANE
    copies = []
    for n, (out, entry, row, dz, target, flip, start, rows, own) in enumerate(plan):
        who = (lane ^ target) if flip else target
        block = order_ref[lax.rem(plane + dz, outer) * PLANE + who]
        low = (group if own else 1 - group) * half + start
        to = outs[out] if entry is None else outs[out].at[entry]
        copies.append(
            pltpu.make_async_copy(
                blocks_ref.at[block, pl.ds(low, rows)], to.at[pl.ds(row, rows)], sems.at[n]
            )
        )
    for n, (out, row) in enumerate(tails):
        for m, part in enumerate((occ_ref, vir_ref)):
            to = outs[out].at[row + m]
            copies.append(pltpu.make_async_copy(part, to, sems.at[len(plan) + 2 * n + m]))
    for copy in copies:
        copy.start()
    for copy in copies:
        copy.wait()


def gather(plan, tails, shapes, outer, half, ri_order, blocks, occupied, virtual):
    size = sum(s.size for s in shapes) * 4
    return pl.pallas_call(
        functools.partial(gather_kernel, plan, tails, outer, half, len(shapes)),
        out_shape=shapes,
        in_specs=[SMEM] + [HBM] * 3,
        out_specs=[VMEM] * len(shapes),
        compiler_params=pltpu.CompilerParams(vmem_limit_bytes=58 * 2**20),
        scratch_shapes=[pltpu.SemaphoreType.DMA((len(plan) + 2 * len(tails),))],
        cost_estimate=pl.CostEstimate(flops=0, bytes_accessed=size, transcendentals=0),
    )(ri_order, blocks, occupied, virtual)


def load(pieces, held, sems, base=0):
    groups = {}
    n = base
    for ref, lead, low, rows, to, at in pieces:
        src = ref if lead is None else ref.at[lead]
        height = src.shape[1]
        for r in range(0, rows, ROWS):
            copy = pltpu.make_async_copy(
                src.at[pl.ds(low + r, ROWS)],
                held.at[pl.ds(to + r, ROWS), pl.ds(at, height)],
                sems.at[n],
            )
            groups.setdefault((to + r) // ROWS, []).append(copy)
            n += 1
    for g in sorted(groups):
        for copy in groups[g]:
            copy.start()
    return groups


def half_step(held, first, occ, vir, keep, mask_t, mix_t, to):
    window = occ.shape[0]
    m = held[first : first + ROWS] * keep[None]
    mask_t[:, to : to + ROWS, :] = jnp.swapaxes(m, 0, 1)
    h = DOT(m.reshape(ROWS * window, window), occ).astype(jnp.bfloat16)
    mixed = [
        DOT(vir, h[p * window : (p + 1) * window]).astype(jnp.bfloat16)[None] for p in range(ROWS)
    ]
    mix_t[:, to : to + ROWS, :] = jnp.swapaxes(jnp.concatenate(mixed), 0, 1)


def front_kernel(places, shifts, outer, orb, count, order_ref, mask_ref, dens_ref, *rest):
    refs = rest[:count]
    mask_t, mix_t, occ_ref, vir_ref, keep_ref, held, sems = rest[count:]
    pieces = [(refs[p[0]],) + p[1:] for p in places]
    groups = load(pieces, held, sems)
    me = lax.axis_index("wide")
    plane, lane = me // PLANE, me % PLANE
    window = occ_ref.shape[0]
    nblk = mask_ref.shape[0]
    block_rows = window // nblk

    def assembled(shape, dim):
        at = lax.broadcasted_iota(jnp.int32, shape, dim)
        place = at // (PLANE * orb)
        device = (at // orb) % PLANE
        source = jnp.zeros(shape, jnp.int32)
        for n, dz in enumerate(shifts):
            who = device if n == outer - 1 else device ^ lane
            from_plane = lax.rem(plane + (outer - dz), outer)
            source = jnp.where(place == n, from_plane * PLANE + who, source)
        return source * orb + at % orb

    arrived = lax.broadcasted_iota(jnp.int32, (window, 2 * window), 1)
    kind = (arrived // orb) % 2
    place = (arrived // (2 * orb)) % outer
    device = (arrived // (2 * orb * outer)) ^ lane
    source = jnp.zeros(arrived.shape, jnp.int32)
    for n, dz in enumerate(shifts):
        from_plane = lax.rem(plane + (outer - dz), outer)
        source = jnp.where(place == n, from_plane * PLANE + device, source)
    orbital = source * orb + arrived % orb
    rows = lax.broadcasted_iota(jnp.int32, (window, 2 * window), 0)
    pick = jnp.where((rows == orbital) & (kind == 0), 1.0, 0.0).astype(jnp.bfloat16)
    dens = dens_ref[...]
    occ = DOT(pick, dens).astype(jnp.bfloat16)
    pick = (assembled((window, 2 * window), 0) == orbital) & (kind == 1)
    pick = jnp.where(pick, 1.0, 0.0).astype(jnp.bfloat16)
    vir = DOT(pick, dens).astype(jnp.bfloat16)
    rows = lax.broadcasted_iota(jnp.int32, (window, window), 0)
    pick = jnp.where(rows == assembled((window, window), 1), 1.0, 0.0).astype(jnp.bfloat16)
    vir = DOT(vir, pick).astype(jnp.bfloat16)
    block = order_ref[me]
    lam = assembled((window, window), 0) // block_rows
    sig = lax.broadcasted_iota(jnp.int32, (window, window), 1) // block_rows
    keep = jnp.zeros((window, window), jnp.int32)
    for a in range(nblk):
        for b in range(nblk):
            keep = jnp.where((lam == a) & (sig == b), mask_ref[a, b, block], keep)
    keep = jnp.where(keep > 0, 1.0, 0.0).astype(jnp.bfloat16)
    occ_ref[...] = occ
    vir_ref[...] = vir
    keep_ref[...] = keep
    for g in sorted(groups):
        for copy in groups[g]:
            copy.wait()
        half_step(held, g * ROWS, occ, vir, keep, mask_t, mix_t, g * ROWS)


def middle_kernel(places, count, occ_ref, vir_ref, keep_ref, *rest):
    refs = rest[:count]
    mask_t, mix_t, held, sems = rest[count:]
    groups = load([(refs[p[0]],) + p[1:] for p in places], held, sems)
    occ, vir, keep = occ_ref[...], vir_ref[...], keep_ref[...]
    for g in sorted(groups):
        for copy in groups[g]:
            copy.wait()
        half_step(held, g * ROWS, occ, vir, keep, mask_t, mix_t, g * ROWS)


def back_kernel(places, count, occ_ref, vir_ref, keep_ref, mask_a, mask_b, mix_a, mix_b, *rest):
    refs = rest[:count]
    out_ref, mask_c, mix_c, held, sems = rest[count:]
    groups = load([(refs[p[0]],) + p[1:] for p in places], held, sems)
    occ, vir, keep = occ_ref[...], vir_ref[...], keep_ref[...]
    for g in sorted(groups):
        for copy in groups[g]:
            copy.wait()
        half_step(held, g * ROWS, occ, vir, keep, mask_c, mix_c, g * ROWS)
    window, rows = mask_c.shape[0], out_ref.shape[0]
    deep = window // CHUNKS

    def body(step, total):
        for k in range(deep):
            m = step * deep + k
            left = jnp.concatenate([mask_a[m], mask_b[m], mask_c[m]])
            right = jnp.concatenate([mix_a[m], mix_b[m], mix_c[m]])
            total += lax.dot_general(
                left, right, (((1,), (1,)), ((), ())), preferred_element_type=jnp.float32
            )
        return total

    total = lax.fori_loop(0, CHUNKS, body, jnp.zeros((rows, rows), jnp.float32))
    half = rows // 2
    turned = jnp.concatenate([total[half:], total[:half]], axis=0)
    turned = jnp.concatenate([turned[:, half:], turned[:, :half]], axis=1)
    out_ref[...] = jnp.where(lax.axis_index("groups") == 0, total, turned)


def shards(tensor, occupied, virtual, block_mask, ri_order):
    wide_count = lax.axis_size("wide")
    outer = wide_count // PLANE
    ri_total, orb, window = tensor.shape
    rows = ri_total // wide_count
    half = rows // 2
    quarter = half // 2
    kind = tensor.dtype
    barrier = lax.optimization_barrier
    planes = [[PLANE * z + i for i in range(PLANE)] for z in range(outer)]

    def inplane(x):
        return lax.all_to_all(
            x, "wide", split_axis=0, concat_axis=0, tiled=True, axis_index_groups=planes
        )

    def shift(x, dz, flip=0):
        pairs = [
            (w, ((w // PLANE + dz) % outer) * PLANE + ((w % PLANE) ^ flip))
            for w in range(wide_count)
        ]
        return lax.ppermute(x, "wide", pairs)

    def swap(x):
        return lax.ppermute(x, "groups", [(0, 1), (1, 0)])

    order = [d for d in range(1, outer) if d != outer // 2] + [outer // 2]
    first, last = order[0], order[-1]
    shape = lambda *s: jax.ShapeDtypeStruct(s + (orb, window), kind)
    blocks = tensor.reshape(wide_count, rows, orb, window)

    def straight(d, at):
        plan = [(at + q, None, 0, d, q, True, 0, half, True) for q in range(PLANE)]
        return plan, [(at, half)], [shape(half + 2)] + [shape(half)] * (PLANE - 1)

    plan, tails, shapes = straight(first, 0)
    pieces = gather(plan, tails, shapes, outer, half, ri_order, blocks, occupied, virtual)
    pieces, held_back = barrier((pieces, blocks))
    plan, tails, shapes = [], [], []
    for d in order[1:-1]:
        more = straight(d, len(shapes))
        plan, tails, shapes = plan + more[0], tails + more[1], shapes + more[2]
    plan += [(len(shapes), i, 0, last, i, False, 0, half, True) for i in range(PLANE)]
    shapes.append(shape(PLANE, half))
    for q in range(PLANE):
        plan += [(len(shapes), None, 0, 0, q, True, 0, half, True)]
        plan += [(len(shapes), None, half, 0, q, True, 0, half, False)]
        shapes.append(shape(rows))
    to_send = gather(plan, tails, shapes, outer, half, ri_order, held_back, occupied, virtual)

    def after(x, other):
        return barrier((x, other))[0]

    direct = list(pieces) + list(to_send[: PLANE * (outer - 3)])
    to_last, near_out = to_send[PLANE * (outer - 3)], to_send[PLANE * (outer - 3) + 1 :]
    base = jnp.stack([occupied, virtual])
    far = shift(base, last)
    came, swapped = [], []
    for n, piece in enumerate(direct):
        if n >= WINDOW:
            piece = after(piece, (came[n - WINDOW], to_last) if n == WINDOW else came[n - WINDOW])
        came.append(shift(piece, order[n // PLANE], n % PLANE))
    ready = inplane(after(to_last, came[1]))
    low = shift(after(ready[:, :quarter], came[-2]), last)
    high = shift(after(ready[:, quarter:], came[-1]), last)
    for n in range(outer - 2):
        group_in = came[PLANE * n : PLANE * (n + 1)]
        swapped.append(swap(jnp.stack([group_in[0][:half]] + group_in[1:])))
    near = [near_out[0]]
    for q in range(1, PLANE):
        near.append(shift(after(near_out[q], near[-1] if q > 1 else came[-PLANE]), 0, q))
    mine = jnp.stack([base] + [came[PLANE * n][half:] for n in range(outer - 2)] + [far])
    dens = [mine] + [shift(mine, 0, q) for q in range(1, PLANE)]
    dens_all = jnp.stack(dens).reshape(2 * window, window)
    swapped.append(swap(low))

    early, front, back = [], [], []
    for i in range(PLANE):
        for n in range(outer):
            at = (n * PLANE + i) * orb
            if n == 0:
                early += [(near[i], None, 0, quarter, 0, at)]
                front += [(near[i], None, quarter, half, 0, at)]
                back += [(near[i], None, half + quarter, quarter, 0, at)]
            elif n < outer - 1:
                early += [(came[PLANE * (n - 1) + i], None, 0, quarter, 0, at)]
                front += [(came[PLANE * (n - 1) + i], None, quarter, quarter, 0, at)]
                front += [(swapped[n - 1], i, 0, quarter, quarter, at)]
                back += [(swapped[n - 1], i, quarter, quarter, 0, at)]
            else:
                early += [(low, i, 0, quarter, 0, at)]
                front += [(high, i, 0, quarter, 0, at)]
                front += [(swapped[-1], i, 0, quarter, quarter, at)]

    def places(listed):
        if orb % ROWS == 0:
            arrays = []
            for p in listed:
                if not any(p[0] is a for a in arrays):
                    arrays.append(p[0])
            number = lambda x: [x is a for a in arrays].index(True)
            return [(number(p[0]),) + p[1:] for p in listed], arrays
        size = max(p[4] + p[3] for p in listed)
        whole = []
        for r in range(0, size, ROWS):
            row = sorted((p for p in listed if p[4] <= r < p[4] + p[3]), key=lambda p: p[5])
            cut = [lax.slice_in_dim(p[0] if p[1] is None else p[0][p[1]], p[2] + r - p[4], p[2] + r - p[4] + ROWS) for p in row]
            whole.append(jnp.concatenate(cut, axis=1))
        return [(0, None, 0, size, 0, 0)], [jnp.concatenate(whole)]

    def copies(table):
        return sum(p[3] // ROWS for p in table)

    params = lambda m: pltpu.CompilerParams(vmem_limit_bytes=m * 2**20)
    mat = jax.ShapeDtypeStruct((window, window), kind)
    tall = lambda n: jax.ShapeDtypeStruct((window, n, window), kind)

    def cost(n, moved):
        return pl.CostEstimate(
            flops=4 * n * window**3, bytes_accessed=moved * window**2, transcendentals=0
        )

    def scratch(n, extra):
        return [
            pltpu.VMEM((n, window, window), kind),
            pltpu.SemaphoreType.DMA((extra,)),
        ]

    rows_of, arrays = places(early)
    mask_a, mix_a, occ, vir, keep = pl.pallas_call(
        functools.partial(front_kernel, rows_of, [0] + order, outer, orb, len(arrays)),
        out_shape=[tall(quarter), tall(quarter), mat, mat, mat],
        in_specs=[SMEM, SMEM, VMEM] + [HBM] * len(arrays),
        out_specs=[VMEM] * 5,
        scratch_shapes=scratch(quarter, copies(rows_of)),
        compiler_params=params(LIM[0]),
        cost_estimate=cost(quarter, 6 * quarter),
    )(ri_order, block_mask.transpose(1, 2, 0), dens_all, *arrays)
    final = swap(after(high, mask_a))
    back += [(final, i, 0, quarter, 0, ((outer - 1) * PLANE + i) * orb) for i in range(PLANE)]
    rows_of, arrays = places(front)
    mask_b, mix_b = pl.pallas_call(
        functools.partial(middle_kernel, rows_of, len(arrays)),
        out_shape=[tall(half), tall(half)],
        in_specs=[VMEM] * 3 + [HBM] * len(arrays),
        out_specs=[VMEM] * 2,
        scratch_shapes=scratch(half, copies(rows_of)),
        compiler_params=params(LIM[1]),
        cost_estimate=cost(half, 6 * half),
    )(occ, vir, keep, *arrays)
    rows_of, arrays = places(back)
    return pl.pallas_call(
        functools.partial(back_kernel, rows_of, len(arrays)),
        out_shape=jax.ShapeDtypeStruct((rows, rows), jnp.float32),
        in_specs=[VMEM] * 7 + [HBM] * len(arrays),
        out_specs=VMEM,
        scratch_shapes=[pltpu.VMEM((window, quarter, window), kind)] * 2
        + scratch(quarter, copies(rows_of)),
        compiler_params=params(LIM[2]),
        cost_estimate=cost(quarter, 4 * rows),
    )(occ, vir, keep, mask_a, mask_b, mix_a, mix_b, *arrays)


def solution(mesh):
    in_specs = (
        P(None, "wide", None),
        P(("groups", "wide"), None),
        P(("groups", "wide"), None),
        P(),
        P(),
    )
    out_specs = P(("groups", "wide"), None)
    return jax.shard_map(shards, mesh=mesh, in_specs=in_specs, out_specs=out_specs, check_vma=False)
```

```python
import functools

import jax
import jax.numpy as jnp
from jax import lax
from jax.experimental import pallas as pl
from jax.experimental.pallas import tpu as pltpu
from jax.sharding import PartitionSpec as P

PLANE = 4
WINDOW = 2
LIM = (16, 24, 28)
CHUNKS = 4
ROWS = 16
VMEM = pl.BlockSpec(memory_space=pltpu.VMEM)
SMEM = pl.BlockSpec(memory_space=pltpu.SMEM)
HBM = pl.BlockSpec(memory_space=pl.ANY)
DOT = functools.partial(jnp.dot, preferred_element_type=jnp.float32)


def gather_kernel(plan, tails, outer, half, count, order_ref, blocks_ref, occ_ref, vir_ref, *rest):
    outs, sems = rest[:count], rest[count]
    me = lax.axis_index("wide")
    group = lax.axis_index("groups")
    plane, lane = me // PLANE, me % PLANE
    copies = []
    for n, (out, entry, row, dz, target, flip, start, rows, own) in enumerate(plan):
        who = (lane ^ target) if flip else target
        block = order_ref[lax.rem(plane + dz, outer) * PLANE + who]
        low = (group if own else 1 - group) * half + start
        to = outs[out] if entry is None else outs[out].at[entry]
        copies.append(
            pltpu.make_async_copy(
                blocks_ref.at[block, pl.ds(low, rows)], to.at[pl.ds(row, rows)], sems.at[n]
            )
        )
    for n, (out, row) in enumerate(tails):
        for m, part in enumerate((occ_ref, vir_ref)):
            to = outs[out].at[row + m]
            copies.append(pltpu.make_async_copy(part, to, sems.at[len(plan) + 2 * n + m]))
    for copy in copies:
        copy.start()
    for copy in copies:
        copy.wait()


def gather(plan, tails, shapes, outer, half, ri_order, blocks, occupied, virtual):
    size = sum(s.size for s in shapes) * 4
    return pl.pallas_call(
        functools.partial(gather_kernel, plan, tails, outer, half, len(shapes)),
        out_shape=shapes,
        in_specs=[SMEM] + [HBM] * 3,
        out_specs=[VMEM] * len(shapes),
        compiler_params=pltpu.CompilerParams(vmem_limit_bytes=58 * 2**20),
        scratch_shapes=[pltpu.SemaphoreType.DMA((len(plan) + 2 * len(tails),))],
        cost_estimate=pl.CostEstimate(flops=0, bytes_accessed=size, transcendentals=0),
    )(ri_order, blocks, occupied, virtual)


def load(pieces, held, sems, base=0):
    groups = {}
    n = base
    for ref, lead, low, rows, to, at in pieces:
        src = ref if lead is None else ref.at[lead]
        height = src.shape[1]
        for r in range(0, rows, ROWS):
            copy = pltpu.make_async_copy(
                src.at[pl.ds(low + r, ROWS)],
                held.at[pl.ds(to + r, ROWS), pl.ds(at, height)],
                sems.at[n],
            )
            groups.setdefault((to + r) // ROWS, []).append(copy)
            n += 1
    for g in sorted(groups):
        for copy in groups[g]:
            copy.start()
    return groups


def half_step(held, first, occ, vir, keep, mask_t, mix_t, to):
    window = occ.shape[0]
    m = held[first : first + ROWS] * keep[None]
    mask_t[:, to : to + ROWS, :] = jnp.swapaxes(m, 0, 1)
    h = DOT(m.reshape(ROWS * window, window), occ).astype(jnp.bfloat16)
    mixed = [
        DOT(vir, h[p * window : (p + 1) * window]).astype(jnp.bfloat16)[None] for p in range(ROWS)
    ]
    mix_t[:, to : to + ROWS, :] = jnp.swapaxes(jnp.concatenate(mixed), 0, 1)


def front_kernel(places, shifts, outer, orb, count, order_ref, mask_ref, dens_ref, *rest):
    refs = rest[:count]
    mask_t, mix_t, occ_ref, vir_ref, keep_ref, held, sems = rest[count:]
    pieces = [(refs[p[0]],) + p[1:] for p in places]
    groups = load(pieces, held, sems)
    me = lax.axis_index("wide")
    plane, lane = me // PLANE, me % PLANE
    window = occ_ref.shape[0]
    nblk = mask_ref.shape[0]
    block_rows = window // nblk

    def assembled(shape, dim):
        at = lax.broadcasted_iota(jnp.int32, shape, dim)
        place = at // (PLANE * orb)
        device = (at // orb) % PLANE
        source = jnp.zeros(shape, jnp.int32)
        for n, dz in enumerate(shifts):
            who = device if n == outer - 1 else device ^ lane
            from_plane = lax.rem(plane + (outer - dz), outer)
            source = jnp.where(place == n, from_plane * PLANE + who, source)
        return source * orb + at % orb

    arrived = lax.broadcasted_iota(jnp.int32, (window, 2 * window), 1)
    kind = (arrived // orb) % 2
    place = (arrived // (2 * orb)) % outer
    device = (arrived // (2 * orb * outer)) ^ lane
    source = jnp.zeros(arrived.shape, jnp.int32)
    for n, dz in enumerate(shifts):
        from_plane = lax.rem(plane + (outer - dz), outer)
        source = jnp.where(place == n, from_plane * PLANE + device, source)
    orbital = source * orb + arrived % orb
    rows = lax.broadcasted_iota(jnp.int32, (window, 2 * window), 0)
    pick = jnp.where((rows == orbital) & (kind == 0), 1.0, 0.0).astype(jnp.bfloat16)
    dens = dens_ref[...]
    occ = DOT(pick, dens).astype(jnp.bfloat16)
    pick = (assembled((window, 2 * window), 0) == orbital) & (kind == 1)
    pick = jnp.where(pick, 1.0, 0.0).astype(jnp.bfloat16)
    vir = DOT(pick, dens).astype(jnp.bfloat16)
    rows = lax.broadcasted_iota(jnp.int32, (window, window), 0)
    pick = jnp.where(rows == assembled((window, window), 1), 1.0, 0.0).astype(jnp.bfloat16)
    vir = DOT(vir, pick).astype(jnp.bfloat16)
    block = order_ref[me]
    lam = assembled((window, window), 0) // block_rows
    sig = lax.broadcasted_iota(jnp.int32, (window, window), 1) // block_rows
    keep = jnp.zeros((window, window), jnp.int32)
    for a in range(nblk):
        for b in range(nblk):
            keep = jnp.where((lam == a) & (sig == b), mask_ref[a, b, block], keep)
    keep = jnp.where(keep > 0, 1.0, 0.0).astype(jnp.bfloat16)
    occ_ref[...] = occ
    vir_ref[...] = vir
    keep_ref[...] = keep
    for g in sorted(groups):
        for copy in groups[g]:
            copy.wait()
        half_step(held, g * ROWS, occ, vir, keep, mask_t, mix_t, g * ROWS)


def middle_kernel(places, count, occ_ref, vir_ref, keep_ref, *rest):
    refs = rest[:count]
    mask_t, mix_t, held, sems = rest[count:]
    groups = load([(refs[p[0]],) + p[1:] for p in places], held, sems)
    occ, vir, keep = occ_ref[...], vir_ref[...], keep_ref[...]
    for g in sorted(groups):
        for copy in groups[g]:
            copy.wait()
        half_step(held, g * ROWS, occ, vir, keep, mask_t, mix_t, g * ROWS)


def back_kernel(places, count, occ_ref, vir_ref, keep_ref, mask_a, mask_b, mix_a, mix_b, *rest):
    refs = rest[:count]
    out_ref, mask_c, mix_c, held, sems = rest[count:]
    groups = load([(refs[p[0]],) + p[1:] for p in places], held, sems)
    occ, vir, keep = occ_ref[...], vir_ref[...], keep_ref[...]
    for g in sorted(groups):
        for copy in groups[g]:
            copy.wait()
        half_step(held, g * ROWS, occ, vir, keep, mask_c, mix_c, g * ROWS)
    window, rows = mask_c.shape[0], out_ref.shape[0]
    deep = window // CHUNKS

    def body(step, total):
        for k in range(deep):
            m = step * deep + k
            left = jnp.concatenate([mask_a[m], mask_b[m], mask_c[m]])
            right = jnp.concatenate([mix_a[m], mix_b[m], mix_c[m]])
            total += lax.dot_general(
                left, right, (((1,), (1,)), ((), ())), preferred_element_type=jnp.float32
            )
        return total

    total = lax.fori_loop(0, CHUNKS, body, jnp.zeros((rows, rows), jnp.float32))
    half = rows // 2
    turned = jnp.concatenate([total[half:], total[:half]], axis=0)
    turned = jnp.concatenate([turned[:, half:], turned[:, :half]], axis=1)
    out_ref[...] = jnp.where(lax.axis_index("groups") == 0, total, turned)


def shards(tensor, occupied, virtual, block_mask, ri_order):
    wide_count = lax.axis_size("wide")
    outer = wide_count // PLANE
    ri_total, orb, window = tensor.shape
    rows = ri_total // wide_count
    half = rows // 2
    quarter = half // 2
    kind = tensor.dtype
    barrier = lax.optimization_barrier
    planes = [[PLANE * z + i for i in range(PLANE)] for z in range(outer)]

    def inplane(x):
        return lax.all_to_all(
            x, "wide", split_axis=0, concat_axis=0, tiled=True, axis_index_groups=planes
        )

    def shift(x, dz, flip=0):
        pairs = [
            (w, ((w // PLANE + dz) % outer) * PLANE + ((w % PLANE) ^ flip))
            for w in range(wide_count)
        ]
        return lax.ppermute(x, "wide", pairs)

    def swap(x):
        return lax.ppermute(x, "groups", [(0, 1), (1, 0)])

    order = [d for d in range(1, outer) if d != outer // 2] + [outer // 2]
    first, last = order[0], order[-1]
    shape = lambda *s: jax.ShapeDtypeStruct(s + (orb, window), kind)
    blocks = tensor.reshape(wide_count, rows, orb, window)

    def straight(d, at):
        plan = [(at + q, None, 0, d, q, True, 0, half, True) for q in range(PLANE)]
        return plan, [(at, half)], [shape(half + 2)] + [shape(half)] * (PLANE - 1)

    plan, tails, shapes = straight(first, 0)
    plan_later, shapes_later = plan[WINDOW:], shapes[WINDOW:]
    pieces = gather(plan[:WINDOW], tails, shapes[:WINDOW], outer, half, ri_order, blocks, occupied, virtual)
    pieces, held_back = barrier((pieces, blocks))
    plan = [(p[0] - WINDOW,) + p[1:] for p in plan_later]
    tails, shapes = [], list(shapes_later)
    for d in order[1:-1]:
        more = straight(d, len(shapes))
        plan, tails, shapes = plan + more[0], tails + more[1], shapes + more[2]
    plan += [(len(shapes), i, 0, last, i, False, 0, half, True) for i in range(PLANE)]
    shapes.append(shape(PLANE, half))
    for q in range(PLANE):
        plan += [(len(shapes), None, 0, 0, q, True, 0, half, True)]
        plan += [(len(shapes), None, half, 0, q, True, 0, half, False)]
        shapes.append(shape(rows))
    to_send = gather(plan, tails, shapes, outer, half, ri_order, held_back, occupied, virtual)

    def after(x, other):
        return barrier((x, other))[0]

    direct = list(pieces) + list(to_send[: PLANE * (outer - 2) - WINDOW])
    to_last, near_out = to_send[-PLANE - 1], to_send[-PLANE:]
    base = jnp.stack([occupied, virtual])
    came, swapped = [], []
    for n, piece in enumerate(direct):
        if n >= WINDOW:
            before = came[n - WINDOW]
            piece = after(piece, (before, to_last) if n == WINDOW else before)
        came.append(shift(piece, order[n // PLANE], n % PLANE))
    ready = inplane(after(to_last, came[1]))
    low = shift(after(ready[:, :quarter], came[-3]), last)
    high = shift(after(ready[:, quarter:], came[-1]), last)
    for n in range(outer - 2):
        group_in = came[PLANE * n : PLANE * (n + 1)]
        swapped.append(swap(jnp.stack([group_in[0][:half]] + group_in[1:])))
    near = [near_out[0]]
    for q in range(1, PLANE):
        near.append(shift(after(near_out[q], near[-1] if q > 1 else came[-PLANE]), 0, q))
    far = shift(base, last)
    mine = jnp.stack([base] + [came[PLANE * n][half:] for n in range(outer - 2)] + [far])
    dens = [mine] + [shift(mine, 0, q) for q in range(1, PLANE)]
    dens_all = jnp.stack(dens).reshape(2 * window, window)
    swapped.append(swap(low))

    early, front, back = [], [], []
    for i in range(PLANE):
        for n in range(outer):
            at = (n * PLANE + i) * orb
            if n == 0:
                early += [(near[i], None, 0, quarter, 0, at)]
                front += [(near[i], None, quarter, half, 0, at)]
                back += [(near[i], None, half + quarter, quarter, 0, at)]
            elif n < outer - 1:
                early += [(came[PLANE * (n - 1) + i], None, 0, quarter, 0, at)]
                front += [(came[PLANE * (n - 1) + i], None, quarter, quarter, 0, at)]
                front += [(swapped[n - 1], i, 0, quarter, quarter, at)]
                back += [(swapped[n - 1], i, quarter, quarter, 0, at)]
            else:
                early += [(low, i, 0, quarter, 0, at)]
                front += [(high, i, 0, quarter, 0, at)]
                front += [(swapped[-1], i, 0, quarter, quarter, at)]

    def places(listed):
        if orb % ROWS == 0:
            arrays = []
            for p in listed:
                if not any(p[0] is a for a in arrays):
                    arrays.append(p[0])
            number = lambda x: [x is a for a in arrays].index(True)
            return [(number(p[0]),) + p[1:] for p in listed], arrays
        size = max(p[4] + p[3] for p in listed)
        whole = []
        for r in range(0, size, ROWS):
            row = sorted((p for p in listed if p[4] <= r < p[4] + p[3]), key=lambda p: p[5])
            cut = [lax.slice_in_dim(p[0] if p[1] is None else p[0][p[1]], p[2] + r - p[4], p[2] + r - p[4] + ROWS) for p in row]
            whole.append(jnp.concatenate(cut, axis=1))
        return [(0, None, 0, size, 0, 0)], [jnp.concatenate(whole)]

    def copies(table):
        return sum(p[3] // ROWS for p in table)

    params = lambda m: pltpu.CompilerParams(vmem_limit_bytes=m * 2**20)
    mat = jax.ShapeDtypeStruct((window, window), kind)
    tall = lambda n: jax.ShapeDtypeStruct((window, n, window), kind)

    def cost(n, moved):
        return pl.CostEstimate(
            flops=4 * n * window**3, bytes_accessed=moved * window**2, transcendentals=0
        )

    def scratch(n, extra):
        return [
            pltpu.VMEM((n, window, window), kind),
            pltpu.SemaphoreType.DMA((extra,)),
        ]

    rows_of, arrays = places(early)
    mask_a, mix_a, occ, vir, keep = pl.pallas_call(
        functools.partial(front_kernel, rows_of, [0] + order, outer, orb, len(arrays)),
        out_shape=[tall(quarter), tall(quarter), mat, mat, mat],
        in_specs=[SMEM, SMEM, VMEM] + [HBM] * len(arrays),
        out_specs=[VMEM] * 5,
        scratch_shapes=scratch(quarter, copies(rows_of)),
        compiler_params=params(LIM[0]),
        cost_estimate=cost(quarter, 6 * quarter),
    )(ri_order, block_mask.transpose(1, 2, 0), dens_all, *arrays)
    final = swap(after(high, mask_a))
    back += [(final, i, 0, quarter, 0, ((outer - 1) * PLANE + i) * orb) for i in range(PLANE)]
    rows_of, arrays = places(front)
    mask_b, mix_b = pl.pallas_call(
        functools.partial(middle_kernel, rows_of, len(arrays)),
        out_shape=[tall(half), tall(half)],
        in_specs=[VMEM] * 3 + [HBM] * len(arrays),
        out_specs=[VMEM] * 2,
        scratch_shapes=scratch(half, copies(rows_of)),
        compiler_params=params(LIM[1]),
        cost_estimate=cost(half, 6 * half),
    )(occ, vir, keep, *arrays)
    rows_of, arrays = places(back)
    return pl.pallas_call(
        functools.partial(back_kernel, rows_of, len(arrays)),
        out_shape=jax.ShapeDtypeStruct((rows, rows), jnp.float32),
        in_specs=[VMEM] * 7 + [HBM] * len(arrays),
        out_specs=VMEM,
        scratch_shapes=[pltpu.VMEM((window, quarter, window), kind)] * 2
        + scratch(quarter, copies(rows_of)),
        compiler_params=params(LIM[2]),
        cost_estimate=cost(quarter, 4 * rows),
    )(occ, vir, keep, mask_a, mask_b, mix_a, mix_b, *arrays)


def solution(mesh):
    in_specs = (
        P(None, "wide", None),
        P(("groups", "wide"), None),
        P(("groups", "wide"), None),
        P(),
        P(),
    )
    out_specs = P(("groups", "wide"), None)
    return jax.shard_map(shards, mesh=mesh, in_specs=in_specs, out_specs=out_specs, check_vma=False)
```

```python
import functools

import jax
import jax.numpy as jnp
from jax import lax
from jax.experimental import pallas as pl
from jax.experimental.pallas import tpu as pltpu
from jax.sharding import PartitionSpec as P

PLANE = 4
WINDOW = 2
LIM = (16, 24, 28)
CHUNKS = 4
ROWS = 16
VMEM = pl.BlockSpec(memory_space=pltpu.VMEM)
SMEM = pl.BlockSpec(memory_space=pltpu.SMEM)
HBM = pl.BlockSpec(memory_space=pl.ANY)
DOT = functools.partial(jnp.dot, preferred_element_type=jnp.float32)


def gather_kernel(plan, tails, outer, half, count, order_ref, blocks_ref, occ_ref, vir_ref, *rest):
    outs, sems = rest[:count], rest[count]
    me = lax.axis_index("wide")
    group = lax.axis_index("groups")
    plane, lane = me // PLANE, me % PLANE
    copies = []
    for n, (out, entry, row, dz, target, flip, start, rows, own) in enumerate(plan):
        who = (lane ^ target) if flip else target
        block = order_ref[lax.rem(plane + dz, outer) * PLANE + who]
        low = (group if own else 1 - group) * half + start
        to = outs[out] if entry is None else outs[out].at[entry]
        copies.append(
            pltpu.make_async_copy(
                blocks_ref.at[block, pl.ds(low, rows)], to.at[pl.ds(row, rows)], sems.at[n]
            )
        )
    for n, (out, row) in enumerate(tails):
        for m, part in enumerate((occ_ref, vir_ref)):
            to = outs[out].at[row + m]
            copies.append(pltpu.make_async_copy(part, to, sems.at[len(plan) + 2 * n + m]))
    for copy in copies:
        copy.start()
    for copy in copies:
        copy.wait()


def gather(plan, tails, shapes, outer, half, ri_order, blocks, occupied, virtual):
    size = sum(s.size for s in shapes) * 4
    return pl.pallas_call(
        functools.partial(gather_kernel, plan, tails, outer, half, len(shapes)),
        out_shape=shapes,
        in_specs=[SMEM] + [HBM] * 3,
        out_specs=[VMEM] * len(shapes),
        compiler_params=pltpu.CompilerParams(vmem_limit_bytes=58 * 2**20),
        scratch_shapes=[pltpu.SemaphoreType.DMA((len(plan) + 2 * len(tails),))],
        cost_estimate=pl.CostEstimate(flops=0, bytes_accessed=size, transcendentals=0),
    )(ri_order, blocks, occupied, virtual)


def load(pieces, held, sems, base=0):
    groups = {}
    n = base
    for ref, lead, low, rows, to, at in pieces:
        src = ref if lead is None else ref.at[lead]
        height = src.shape[1]
        for r in range(0, rows, ROWS):
            copy = pltpu.make_async_copy(
                src.at[pl.ds(low + r, ROWS)],
                held.at[pl.ds(to + r, ROWS), pl.ds(at, height)],
                sems.at[n],
            )
            groups.setdefault((to + r) // ROWS, []).append(copy)
            n += 1
    for g in sorted(groups):
        for copy in groups[g]:
            copy.start()
    return groups


def half_step(held, first, occ, vir, keep, mask_t, mix_t, to):
    window = occ.shape[0]
    m = held[first : first + ROWS] * keep[None]
    mask_t[:, to : to + ROWS, :] = jnp.swapaxes(m, 0, 1)
    h = DOT(m.reshape(ROWS * window, window), occ).astype(jnp.bfloat16)
    mixed = [
        DOT(vir, h[p * window : (p + 1) * window]).astype(jnp.bfloat16)[None] for p in range(ROWS)
    ]
    mix_t[:, to : to + ROWS, :] = jnp.swapaxes(jnp.concatenate(mixed), 0, 1)


def front_kernel(places, shifts, outer, orb, count, order_ref, mask_ref, dens_ref, *rest):
    refs = rest[:count]
    mask_t, mix_t, occ_ref, vir_ref, keep_ref, held, sems = rest[count:]
    pieces = [(refs[p[0]],) + p[1:] for p in places]
    groups = load(pieces, held, sems)
    me = lax.axis_index("wide")
    plane, lane = me // PLANE, me % PLANE
    window = occ_ref.shape[0]
    nblk = mask_ref.shape[0]
    block_rows = window // nblk

    def assembled(shape, dim):
        at = lax.broadcasted_iota(jnp.int32, shape, dim)
        place = at // (PLANE * orb)
        device = (at // orb) % PLANE
        source = jnp.zeros(shape, jnp.int32)
        for n, dz in enumerate(shifts):
            who = device if n == outer - 1 else device ^ lane
            from_plane = lax.rem(plane + (outer - dz), outer)
            source = jnp.where(place == n, from_plane * PLANE + who, source)
        return source * orb + at % orb

    arrived = lax.broadcasted_iota(jnp.int32, (window, 2 * window), 1)
    kind = (arrived // orb) % 2
    place = (arrived // (2 * orb)) % outer
    device = (arrived // (2 * orb * outer)) ^ lane
    source = jnp.zeros(arrived.shape, jnp.int32)
    for n, dz in enumerate(shifts):
        from_plane = lax.rem(plane + (outer - dz), outer)
        source = jnp.where(place == n, from_plane * PLANE + device, source)
    orbital = source * orb + arrived % orb
    rows = lax.broadcasted_iota(jnp.int32, (window, 2 * window), 0)
    pick = jnp.where((rows == orbital) & (kind == 0), 1.0, 0.0).astype(jnp.bfloat16)
    dens = dens_ref[...]
    occ = DOT(pick, dens).astype(jnp.bfloat16)
    pick = (assembled((window, 2 * window), 0) == orbital) & (kind == 1)
    pick = jnp.where(pick, 1.0, 0.0).astype(jnp.bfloat16)
    vir = DOT(pick, dens).astype(jnp.bfloat16)
    rows = lax.broadcasted_iota(jnp.int32, (window, window), 0)
    pick = jnp.where(rows == assembled((window, window), 1), 1.0, 0.0).astype(jnp.bfloat16)
    vir = DOT(vir, pick).astype(jnp.bfloat16)
    block = order_ref[me]
    lam = assembled((window, window), 0) // block_rows
    sig = lax.broadcasted_iota(jnp.int32, (window, window), 1) // block_rows
    keep = jnp.zeros((window, window), jnp.int32)
    for a in range(nblk):
        for b in range(nblk):
            keep = jnp.where((lam == a) & (sig == b), mask_ref[a, b, block], keep)
    keep = jnp.where(keep > 0, 1.0, 0.0).astype(jnp.bfloat16)
    occ_ref[...] = occ
    vir_ref[...] = vir
    keep_ref[...] = keep
    for g in sorted(groups):
        for copy in groups[g]:
            copy.wait()
        half_step(held, g * ROWS, occ, vir, keep, mask_t, mix_t, g * ROWS)


def middle_kernel(places, count, occ_ref, vir_ref, keep_ref, *rest):
    refs = rest[:count]
    mask_t, mix_t, held, sems = rest[count:]
    groups = load([(refs[p[0]],) + p[1:] for p in places], held, sems)
    occ, vir, keep = occ_ref[...], vir_ref[...], keep_ref[...]
    for g in sorted(groups):
        for copy in groups[g]:
            copy.wait()
        half_step(held, g * ROWS, occ, vir, keep, mask_t, mix_t, g * ROWS)


def back_kernel(places, count, occ_ref, vir_ref, keep_ref, mask_a, mask_b, mix_a, mix_b, *rest):
    refs = rest[:count]
    out_ref, mask_c, mix_c, held, sems = rest[count:]
    groups = load([(refs[p[0]],) + p[1:] for p in places], held, sems)
    occ, vir, keep = occ_ref[...], vir_ref[...], keep_ref[...]
    for g in sorted(groups):
        for copy in groups[g]:
            copy.wait()
        half_step(held, g * ROWS, occ, vir, keep, mask_c, mix_c, g * ROWS)
    window, rows = mask_c.shape[0], out_ref.shape[0]
    deep = window // CHUNKS

    def body(step, total):
        for k in range(deep):
            m = step * deep + k
            left = jnp.concatenate([mask_a[m], mask_b[m], mask_c[m]])
            right = jnp.concatenate([mix_a[m], mix_b[m], mix_c[m]])
            total += lax.dot_general(
                left, right, (((1,), (1,)), ((), ())), preferred_element_type=jnp.float32
            )
        return total

    total = lax.fori_loop(0, CHUNKS, body, jnp.zeros((rows, rows), jnp.float32))
    half = rows // 2
    turned = jnp.concatenate([total[half:], total[:half]], axis=0)
    turned = jnp.concatenate([turned[:, half:], turned[:, :half]], axis=1)
    out_ref[...] = jnp.where(lax.axis_index("groups") == 0, total, turned)


def shards(tensor, occupied, virtual, block_mask, ri_order):
    wide_count = lax.axis_size("wide")
    outer = wide_count // PLANE
    ri_total, orb, window = tensor.shape
    rows = ri_total // wide_count
    half = rows // 2
    quarter = half // 2
    kind = tensor.dtype
    barrier = lax.optimization_barrier
    planes = [[PLANE * z + i for i in range(PLANE)] for z in range(outer)]

    def inplane(x):
        return lax.all_to_all(
            x, "wide", split_axis=0, concat_axis=0, tiled=True, axis_index_groups=planes
        )

    def shift(x, dz, flip=0):
        pairs = [
            (w, ((w // PLANE + dz) % outer) * PLANE + ((w % PLANE) ^ flip))
            for w in range(wide_count)
        ]
        return lax.ppermute(x, "wide", pairs)

    def swap(x):
        return lax.ppermute(x, "groups", [(0, 1), (1, 0)])

    order = [d for d in range(1, outer) if d != outer // 2] + [outer // 2]
    first, last = order[0], order[-1]
    shape = lambda *s: jax.ShapeDtypeStruct(s + (orb, window), kind)
    blocks = tensor.reshape(wide_count, rows, orb, window)

    def straight(d, at):
        plan = [(at + q, None, 0, d, q, True, 0, half, True) for q in range(PLANE)]
        return plan, [(at, half)], [shape(half + 2)] + [shape(half)] * (PLANE - 1)

    plan, tails, shapes = straight(first, 0)
    plan_later, shapes_later = plan[WINDOW:], shapes[WINDOW:]
    pieces = gather(plan[:WINDOW], tails, shapes[:WINDOW], outer, half, ri_order, blocks, occupied, virtual)
    pieces, held_back = barrier((pieces, blocks))
    plan = [(p[0] - WINDOW,) + p[1:] for p in plan_later]
    tails, shapes = [], list(shapes_later)
    for d in order[1:-1]:
        more = straight(d, len(shapes))
        plan, tails, shapes = plan + more[0], tails + more[1], shapes + more[2]
    plan += [(len(shapes), i, 0, last, i, False, 0, half, True) for i in range(PLANE)]
    shapes.append(shape(PLANE, half))
    for q in range(PLANE):
        plan += [(len(shapes), None, 0, 0, q, True, 0, half, True)]
        plan += [(len(shapes), None, half, 0, q, True, 0, half, False)]
        shapes.append(shape(rows))
    to_send = gather(plan, tails, shapes, outer, half, ri_order, held_back, occupied, virtual)

    def after(x, other):
        return barrier((x, other))[0]

    direct = list(pieces) + list(to_send[: PLANE * (outer - 2) - WINDOW])
    to_last, near_out = to_send[-PLANE - 1], to_send[-PLANE:]
    base = jnp.stack([occupied, virtual])
    came, swapped = [], []
    came = [None] * len(direct)
    row = [PLANE * (n // PLANE) + (1, 0, 3, 2, 1, 0, 3, 2)[n % 8] for n in range(len(direct))]
    for n, at in enumerate(row):
        piece = direct[at]
        if n >= WINDOW:
            before = came[row[n - WINDOW]]
            piece = after(piece, (before, to_last) if n == WINDOW else before)
        came[at] = shift(piece, order[at // PLANE], at % PLANE)
    ready = inplane(after(to_last, came[row[1]]))
    low = shift(after(ready[:, :quarter], came[row[-3]]), last)
    high = shift(after(ready[:, quarter:], came[row[-2]]), last)
    for n in range(outer - 2):
        group_in = came[PLANE * n : PLANE * (n + 1)]
        swapped.append(swap(jnp.stack([group_in[0][:half]] + group_in[1:])))
    near = [near_out[0]]
    for q in range(1, PLANE):
        near.append(shift(after(near_out[q], near[-1] if q > 1 else came[row[-PLANE]]), 0, q))
    far = shift(base, last)
    mine = jnp.stack([base] + [came[PLANE * n][half:] for n in range(outer - 2)] + [far])
    dens = [mine] + [shift(mine, 0, q) for q in range(1, PLANE)]
    dens_all = jnp.stack(dens).reshape(2 * window, window)
    swapped.append(swap(low))

    early, front, back = [], [], []
    for i in range(PLANE):
        for n in range(outer):
            at = (n * PLANE + i) * orb
            if n == 0:
                early += [(near[i], None, 0, quarter, 0, at)]
                front += [(near[i], None, quarter, half, 0, at)]
                back += [(near[i], None, half + quarter, quarter, 0, at)]
            elif n < outer - 1:
                early += [(came[PLANE * (n - 1) + i], None, 0, quarter, 0, at)]
                front += [(came[PLANE * (n - 1) + i], None, quarter, quarter, 0, at)]
                front += [(swapped[n - 1], i, 0, quarter, quarter, at)]
                back += [(swapped[n - 1], i, quarter, quarter, 0, at)]
            else:
                early += [(low, i, 0, quarter, 0, at)]
                front += [(high, i, 0, quarter, 0, at)]
                front += [(swapped[-1], i, 0, quarter, quarter, at)]

    def places(listed):
        if orb % ROWS == 0:
            arrays = []
            for p in listed:
                if not any(p[0] is a for a in arrays):
                    arrays.append(p[0])
            number = lambda x: [x is a for a in arrays].index(True)
            return [(number(p[0]),) + p[1:] for p in listed], arrays
        size = max(p[4] + p[3] for p in listed)
        whole = []
        for r in range(0, size, ROWS):
            row = sorted((p for p in listed if p[4] <= r < p[4] + p[3]), key=lambda p: p[5])
            cut = [lax.slice_in_dim(p[0] if p[1] is None else p[0][p[1]], p[2] + r - p[4], p[2] + r - p[4] + ROWS) for p in row]
            whole.append(jnp.concatenate(cut, axis=1))
        return [(0, None, 0, size, 0, 0)], [jnp.concatenate(whole)]

    def copies(table):
        return sum(p[3] // ROWS for p in table)

    params = lambda m: pltpu.CompilerParams(vmem_limit_bytes=m * 2**20)
    mat = jax.ShapeDtypeStruct((window, window), kind)
    tall = lambda n: jax.ShapeDtypeStruct((window, n, window), kind)

    def cost(n, moved):
        return pl.CostEstimate(
            flops=4 * n * window**3, bytes_accessed=moved * window**2, transcendentals=0
        )

    def scratch(n, extra):
        return [
            pltpu.VMEM((n, window, window), kind),
            pltpu.SemaphoreType.DMA((extra,)),
        ]

    rows_of, arrays = places(early)
    mask_a, mix_a, occ, vir, keep = pl.pallas_call(
        functools.partial(front_kernel, rows_of, [0] + order, outer, orb, len(arrays)),
        out_shape=[tall(quarter), tall(quarter), mat, mat, mat],
        in_specs=[SMEM, SMEM, VMEM] + [HBM] * len(arrays),
        out_specs=[VMEM] * 5,
        scratch_shapes=scratch(quarter, copies(rows_of)),
        compiler_params=params(LIM[0]),
        cost_estimate=cost(quarter, 6 * quarter),
    )(ri_order, block_mask.transpose(1, 2, 0), dens_all, *arrays)
    final = swap(after(high, mask_a))
    back += [(final, i, 0, quarter, 0, ((outer - 1) * PLANE + i) * orb) for i in range(PLANE)]
    rows_of, arrays = places(front)
    mask_b, mix_b = pl.pallas_call(
        functools.partial(middle_kernel, rows_of, len(arrays)),
        out_shape=[tall(half), tall(half)],
        in_specs=[VMEM] * 3 + [HBM] * len(arrays),
        out_specs=[VMEM] * 2,
        scratch_shapes=scratch(half, copies(rows_of)),
        compiler_params=params(LIM[1]),
        cost_estimate=cost(half, 6 * half),
    )(occ, vir, keep, *arrays)
    rows_of, arrays = places(back)
    return pl.pallas_call(
        functools.partial(back_kernel, rows_of, len(arrays)),
        out_shape=jax.ShapeDtypeStruct((rows, rows), jnp.float32),
        in_specs=[VMEM] * 7 + [HBM] * len(arrays),
        out_specs=VMEM,
        scratch_shapes=[pltpu.VMEM((window, quarter, window), kind)] * 2
        + scratch(quarter, copies(rows_of)),
        compiler_params=params(LIM[2]),
        cost_estimate=cost(quarter, 4 * rows),
    )(occ, vir, keep, mask_a, mask_b, mix_a, mix_b, *arrays)


def solution(mesh):
    in_specs = (
        P(None, "wide", None),
        P(("groups", "wide"), None),
        P(("groups", "wide"), None),
        P(),
        P(),
    )
    out_specs = P(("groups", "wide"), None)
    return jax.shard_map(shards, mesh=mesh, in_specs=in_specs, out_specs=out_specs, check_vma=False)
```

```python
import functools

import jax
import jax.numpy as jnp
from jax import lax
from jax.experimental import pallas as pl
from jax.experimental.pallas import tpu as pltpu
from jax.sharding import PartitionSpec as P

PLANE = 4
WINDOW = 2
LIM = (16, 24, 28)
CHUNKS = 4
ROWS = 16
VMEM = pl.BlockSpec(memory_space=pltpu.VMEM)
SMEM = pl.BlockSpec(memory_space=pltpu.SMEM)
HBM = pl.BlockSpec(memory_space=pl.ANY)
DOT = functools.partial(jnp.dot, preferred_element_type=jnp.float32)


def gather_kernel(plan, tails, outer, half, count, order_ref, blocks_ref, occ_ref, vir_ref, *rest):
    outs, sems = rest[:count], rest[count]
    me = lax.axis_index("wide")
    group = lax.axis_index("groups")
    plane, lane = me // PLANE, me % PLANE
    copies = []
    for n, (out, entry, row, dz, target, flip, start, rows, own) in enumerate(plan):
        who = (lane ^ target) if flip else target
        block = order_ref[lax.rem(plane + dz, outer) * PLANE + who]
        low = (group if own else 1 - group) * half + start
        to = outs[out] if entry is None else outs[out].at[entry]
        copies.append(
            pltpu.make_async_copy(
                blocks_ref.at[block, pl.ds(low, rows)], to.at[pl.ds(row, rows)], sems.at[n]
            )
        )
    for n, (out, row) in enumerate(tails):
        for m, part in enumerate((occ_ref, vir_ref)):
            to = outs[out].at[row + m]
            copies.append(pltpu.make_async_copy(part, to, sems.at[len(plan) + 2 * n + m]))
    for copy in copies:
        copy.start()
    for copy in copies:
        copy.wait()


def gather(plan, tails, shapes, outer, half, ri_order, blocks, occupied, virtual):
    size = sum(s.size for s in shapes) * 4
    return pl.pallas_call(
        functools.partial(gather_kernel, plan, tails, outer, half, len(shapes)),
        out_shape=shapes,
        in_specs=[SMEM] + [HBM] * 3,
        out_specs=[VMEM] * len(shapes),
        compiler_params=pltpu.CompilerParams(vmem_limit_bytes=58 * 2**20),
        scratch_shapes=[pltpu.SemaphoreType.DMA((len(plan) + 2 * len(tails),))],
        cost_estimate=pl.CostEstimate(flops=0, bytes_accessed=size, transcendentals=0),
    )(ri_order, blocks, occupied, virtual)


def load(pieces, held, sems, base=0):
    groups = {}
    n = base
    for ref, lead, low, rows, to, at in pieces:
        src = ref if lead is None else ref.at[lead]
        height = src.shape[1]
        for r in range(0, rows, ROWS):
            copy = pltpu.make_async_copy(
                src.at[pl.ds(low + r, ROWS)],
                held.at[pl.ds(to + r, ROWS), pl.ds(at, height)],
                sems.at[n],
            )
            groups.setdefault((to + r) // ROWS, []).append(copy)
            n += 1
    for g in sorted(groups):
        for copy in groups[g]:
            copy.start()
    return groups


def half_step(held, first, occ, vir, keep, mask_t, mix_t, to):
    window = occ.shape[0]
    m = held[first : first + ROWS] * keep[None]
    mask_t[:, to : to + ROWS, :] = jnp.swapaxes(m, 0, 1)
    h = DOT(m.reshape(ROWS * window, window), occ).astype(jnp.bfloat16)
    mixed = [
        DOT(vir, h[p * window : (p + 1) * window]).astype(jnp.bfloat16)[None] for p in range(ROWS)
    ]
    mix_t[:, to : to + ROWS, :] = jnp.swapaxes(jnp.concatenate(mixed), 0, 1)


def front_kernel(places, shifts, outer, orb, count, order_ref, mask_ref, dens_ref, *rest):
    refs = rest[:count]
    mask_t, mix_t, occ_ref, vir_ref, keep_ref, held, sems = rest[count:]
    pieces = [(refs[p[0]],) + p[1:] for p in places]
    groups = load(pieces, held, sems)
    me = lax.axis_index("wide")
    plane, lane = me // PLANE, me % PLANE
    window = occ_ref.shape[0]
    nblk = mask_ref.shape[0]
    block_rows = window // nblk

    def assembled(shape, dim):
        at = lax.broadcasted_iota(jnp.int32, shape, dim)
        place = at // (PLANE * orb)
        device = (at // orb) % PLANE
        source = jnp.zeros(shape, jnp.int32)
        for n, dz in enumerate(shifts):
            who = device if n == outer - 1 else device ^ lane
            from_plane = lax.rem(plane + (outer - dz), outer)
            source = jnp.where(place == n, from_plane * PLANE + who, source)
        return source * orb + at % orb

    arrived = lax.broadcasted_iota(jnp.int32, (window, 2 * window), 1)
    kind = (arrived // orb) % 2
    place = (arrived // (2 * orb)) % outer
    device = (arrived // (2 * orb * outer)) ^ lane
    source = jnp.zeros(arrived.shape, jnp.int32)
    for n, dz in enumerate(shifts):
        from_plane = lax.rem(plane + (outer - dz), outer)
        source = jnp.where(place == n, from_plane * PLANE + device, source)
    orbital = source * orb + arrived % orb
    rows = lax.broadcasted_iota(jnp.int32, (window, 2 * window), 0)
    pick = jnp.where((rows == orbital) & (kind == 0), 1.0, 0.0).astype(jnp.bfloat16)
    dens = dens_ref[...]
    occ = DOT(pick, dens).astype(jnp.bfloat16)
    pick = (assembled((window, 2 * window), 0) == orbital) & (kind == 1)
    pick = jnp.where(pick, 1.0, 0.0).astype(jnp.bfloat16)
    vir = DOT(pick, dens).astype(jnp.bfloat16)
    rows = lax.broadcasted_iota(jnp.int32, (window, window), 0)
    pick = jnp.where(rows == assembled((window, window), 1), 1.0, 0.0).astype(jnp.bfloat16)
    vir = DOT(vir, pick).astype(jnp.bfloat16)
    block = order_ref[me]
    lam = assembled((window, window), 0) // block_rows
    sig = lax.broadcasted_iota(jnp.int32, (window, window), 1) // block_rows
    keep = jnp.zeros((window, window), jnp.int32)
    for a in range(nblk):
        for b in range(nblk):
            keep = jnp.where((lam == a) & (sig == b), mask_ref[a, b, block], keep)
    keep = jnp.where(keep > 0, 1.0, 0.0).astype(jnp.bfloat16)
    occ_ref[...] = occ
    vir_ref[...] = vir
    keep_ref[...] = keep
    for g in sorted(groups):
        for copy in groups[g]:
            copy.wait()
        half_step(held, g * ROWS, occ, vir, keep, mask_t, mix_t, g * ROWS)


def middle_kernel(places, count, occ_ref, vir_ref, keep_ref, *rest):
    refs = rest[:count]
    mask_t, mix_t, held, sems = rest[count:]
    groups = load([(refs[p[0]],) + p[1:] for p in places], held, sems)
    occ, vir, keep = occ_ref[...], vir_ref[...], keep_ref[...]
    for g in sorted(groups):
        for copy in groups[g]:
            copy.wait()
        half_step(held, g * ROWS, occ, vir, keep, mask_t, mix_t, g * ROWS)


def back_kernel(places, count, occ_ref, vir_ref, keep_ref, mask_a, mask_b, mix_a, mix_b, *rest):
    refs = rest[:count]
    out_ref, mask_c, mix_c, held, sems = rest[count:]
    groups = load([(refs[p[0]],) + p[1:] for p in places], held, sems)
    occ, vir, keep = occ_ref[...], vir_ref[...], keep_ref[...]
    for g in sorted(groups):
        for copy in groups[g]:
            copy.wait()
        half_step(held, g * ROWS, occ, vir, keep, mask_c, mix_c, g * ROWS)
    window, rows = mask_c.shape[0], out_ref.shape[0]
    deep = window // CHUNKS

    def body(step, total):
        for k in range(deep):
            m = step * deep + k
            left = jnp.concatenate([mask_a[m], mask_b[m], mask_c[m]])
            right = jnp.concatenate([mix_a[m], mix_b[m], mix_c[m]])
            total += lax.dot_general(
                left, right, (((1,), (1,)), ((), ())), preferred_element_type=jnp.float32
            )
        return total

    total = lax.fori_loop(0, CHUNKS, body, jnp.zeros((rows, rows), jnp.float32))
    half = rows // 2
    turned = jnp.concatenate([total[half:], total[:half]], axis=0)
    turned = jnp.concatenate([turned[:, half:], turned[:, :half]], axis=1)
    out_ref[...] = jnp.where(lax.axis_index("groups") == 0, total, turned)


def shards(tensor, occupied, virtual, block_mask, ri_order):
    wide_count = lax.axis_size("wide")
    outer = wide_count // PLANE
    ri_total, orb, window = tensor.shape
    rows = ri_total // wide_count
    half = rows // 2
    quarter = half // 2
    kind = tensor.dtype
    barrier = lax.optimization_barrier
    planes = [[PLANE * z + i for i in range(PLANE)] for z in range(outer)]

    def inplane(x):
        return lax.all_to_all(
            x, "wide", split_axis=0, concat_axis=0, tiled=True, axis_index_groups=planes
        )

    def shift(x, dz, flip=0):
        pairs = [
            (w, ((w // PLANE + dz) % outer) * PLANE + ((w % PLANE) ^ flip))
            for w in range(wide_count)
        ]
        return lax.ppermute(x, "wide", pairs)

    def swap(x):
        return lax.ppermute(x, "groups", [(0, 1), (1, 0)])

    order = [d for d in range(1, outer) if d != outer // 2] + [outer // 2]
    first, last = order[0], order[-1]
    shape = lambda *s: jax.ShapeDtypeStruct(s + (orb, window), kind)
    blocks = tensor.reshape(wide_count, rows, orb, window)

    def straight(d, at):
        plan = [(at + q, None, 0, d, q, True, 0, half, True) for q in range(PLANE)]
        return plan, [(at, half)], [shape(half + 2)] + [shape(half)] * (PLANE - 1)

    plan, tails, shapes = straight(first, 0)
    plan_later, shapes_later = plan[WINDOW:], shapes[WINDOW:]
    pieces = gather(plan[:WINDOW], tails, shapes[:WINDOW], outer, half, ri_order, blocks, occupied, virtual)
    pieces, held_back = barrier((pieces, blocks))
    plan = [(p[0] - WINDOW,) + p[1:] for p in plan_later]
    tails, shapes = [], list(shapes_later)
    for d in order[1:-1]:
        more = straight(d, len(shapes))
        plan, tails, shapes = plan + more[0], tails + more[1], shapes + more[2]
    plan += [(len(shapes), i, 0, last, i, False, 0, half, True) for i in range(PLANE)]
    shapes.append(shape(PLANE, half))
    for q in range(PLANE):
        plan += [(len(shapes), None, 0, 0, q, True, 0, half, True)]
        plan += [(len(shapes), None, half, 0, q, True, 0, half, False)]
        shapes.append(shape(rows))
    to_send = gather(plan, tails, shapes, outer, half, ri_order, held_back, occupied, virtual)

    def after(x, other):
        return barrier((x, other))[0]

    direct = list(pieces) + list(to_send[: PLANE * (outer - 2) - WINDOW])
    to_last, near_out = to_send[-PLANE - 1], to_send[-PLANE:]
    base = jnp.stack([occupied, virtual])
    came, swapped = [], []
    came = [None] * len(direct)
    row = [PLANE * (n // PLANE) + (0, 1, 3, 2, 0, 3, 2, 1)[n % 8] for n in range(len(direct))]
    for n, at in enumerate(row):
        piece = direct[at]
        if n >= WINDOW:
            before = came[row[n - WINDOW]]
            piece = after(piece, (before, to_last) if n == WINDOW else before)
        came[at] = shift(piece, order[at // PLANE], at % PLANE)
    ready = inplane(after(to_last, came[row[1]]))
    low = shift(after(ready[:, :quarter], came[row[-3]]), last)
    high = shift(after(ready[:, quarter:], came[row[-2]]), last)
    for n in range(outer - 2):
        group_in = came[PLANE * n : PLANE * (n + 1)]
        swapped.append(swap(jnp.stack([group_in[0][:half]] + group_in[1:])))
    near = [near_out[0]]
    for q in range(1, PLANE):
        near.append(shift(after(near_out[q], near[-1] if q > 1 else came[row[-PLANE]]), 0, q))
    far = shift(base, last)
    mine = jnp.stack([base] + [came[PLANE * n][half:] for n in range(outer - 2)] + [far])
    dens = [mine] + [shift(mine, 0, q) for q in range(1, PLANE)]
    dens_all = jnp.stack(dens).reshape(2 * window, window)
    swapped.append(swap(low))

    early, front, back = [], [], []
    for i in range(PLANE):
        for n in range(outer):
            at = (n * PLANE + i) * orb
            if n == 0:
                early += [(near[i], None, 0, quarter, 0, at)]
                front += [(near[i], None, quarter, half, 0, at)]
                back += [(near[i], None, half + quarter, quarter, 0, at)]
            elif n < outer - 1:
                early += [(came[PLANE * (n - 1) + i], None, 0, quarter, 0, at)]
                front += [(came[PLANE * (n - 1) + i], None, quarter, quarter, 0, at)]
                front += [(swapped[n - 1], i, 0, quarter, quarter, at)]
                back += [(swapped[n - 1], i, quarter, quarter, 0, at)]
            else:
                early += [(low, i, 0, quarter, 0, at)]
                front += [(high, i, 0, quarter, 0, at)]
                front += [(swapped[-1], i, 0, quarter, quarter, at)]

    def places(listed):
        if orb % ROWS == 0:
            arrays = []
            for p in listed:
                if not any(p[0] is a for a in arrays):
                    arrays.append(p[0])
            number = lambda x: [x is a for a in arrays].index(True)
            return [(number(p[0]),) + p[1:] for p in listed], arrays
        size = max(p[4] + p[3] for p in listed)
        whole = []
        for r in range(0, size, ROWS):
            row = sorted((p for p in listed if p[4] <= r < p[4] + p[3]), key=lambda p: p[5])
            cut = [lax.slice_in_dim(p[0] if p[1] is None else p[0][p[1]], p[2] + r - p[4], p[2] + r - p[4] + ROWS) for p in row]
            whole.append(jnp.concatenate(cut, axis=1))
        return [(0, None, 0, size, 0, 0)], [jnp.concatenate(whole)]

    def copies(table):
        return sum(p[3] // ROWS for p in table)

    params = lambda m: pltpu.CompilerParams(vmem_limit_bytes=m * 2**20)
    mat = jax.ShapeDtypeStruct((window, window), kind)
    tall = lambda n: jax.ShapeDtypeStruct((window, n, window), kind)

    def cost(n, moved):
        return pl.CostEstimate(
            flops=4 * n * window**3, bytes_accessed=moved * window**2, transcendentals=0
        )

    def scratch(n, extra):
        return [
            pltpu.VMEM((n, window, window), kind),
            pltpu.SemaphoreType.DMA((extra,)),
        ]

    rows_of, arrays = places(early)
    mask_a, mix_a, occ, vir, keep = pl.pallas_call(
        functools.partial(front_kernel, rows_of, [0] + order, outer, orb, len(arrays)),
        out_shape=[tall(quarter), tall(quarter), mat, mat, mat],
        in_specs=[SMEM, SMEM, VMEM] + [HBM] * len(arrays),
        out_specs=[VMEM] * 5,
        scratch_shapes=scratch(quarter, copies(rows_of)),
        compiler_params=params(LIM[0]),
        cost_estimate=cost(quarter, 6 * quarter),
    )(ri_order, block_mask.transpose(1, 2, 0), dens_all, *arrays)
    final = swap(after(high, mask_a))
    back += [(final, i, 0, quarter, 0, ((outer - 1) * PLANE + i) * orb) for i in range(PLANE)]
    rows_of, arrays = places(front)
    mask_b, mix_b = pl.pallas_call(
        functools.partial(middle_kernel, rows_of, len(arrays)),
        out_shape=[tall(half), tall(half)],
        in_specs=[VMEM] * 3 + [HBM] * len(arrays),
        out_specs=[VMEM] * 2,
        scratch_shapes=scratch(half, copies(rows_of)),
        compiler_params=params(LIM[1]),
        cost_estimate=cost(half, 6 * half),
    )(occ, vir, keep, *arrays)
    rows_of, arrays = places(back)
    return pl.pallas_call(
        functools.partial(back_kernel, rows_of, len(arrays)),
        out_shape=jax.ShapeDtypeStruct((rows, rows), jnp.float32),
        in_specs=[VMEM] * 7 + [HBM] * len(arrays),
        out_specs=VMEM,
        scratch_shapes=[pltpu.VMEM((window, quarter, window), kind)] * 2
        + scratch(quarter, copies(rows_of)),
        compiler_params=params(LIM[2]),
        cost_estimate=cost(quarter, 4 * rows),
    )(occ, vir, keep, mask_a, mask_b, mix_a, mix_b, *arrays)


def solution(mesh):
    in_specs = (
        P(None, "wide", None),
        P(("groups", "wide"), None),
        P(("groups", "wide"), None),
        P(),
        P(),
    )
    out_specs = P(("groups", "wide"), None)
    return jax.shard_map(shards, mesh=mesh, in_specs=in_specs, out_specs=out_specs, check_vma=False)
```
